128 devices in a mesh: zone: 16 (over x, z), tile: 8 (over y, core).
Axes of the slice: x: 4, y: 4, z: 4, core: 2. Of those that a mesh axis runs over, the one named last changes fastest.
Arguments:
- a_coord: float32 [2, 4194304], P(None, ('zone', 'tile')), may hold values from -6 to 6
- a_var: float32 [4194304], P(('zone', 'tile')), may hold values from 0.1 to 1
- dest: int32 [32768, 1], P(('zone', 'tile')), may hold values from 0 to 127; in each aligned block of 256 rows (0 to 255, 256 to 511, ...) at most 4 rows name the same one
- cand: int32 [32768, 4], P(('zone', 'tile')), may hold values from 0 to 79
- cand_count: int32 [32768, 1], P(('zone', 'tile')), may hold values from 1 to 4
- b_coord: float32 [2, 1048576], P(None, ('zone', 'tile')), may hold values from -6 to 6
- b_var: float32 [1048576], P(('zone', 'tile')), may hold values from 0.1 to 1
- b_prior: float32 [1048576], P(('zone', 'tile')), may hold values from 0.002 to 0.02
- b_flux: float32 [3, 1048576], P(None, ('zone', 'tile')), may hold values from -6 to 6
Outputs:
- matched: float32 [5, 4194304], P(None, ('zone', 'tile'))
- match_prob: float32 [4194304], P(('zone', 'tile'))
The draws below stay inside these ranges and needn't reach their ends.
Inputs may be any that keep to these rules, and one draw needn't show every extreme that they name: `dest`: among the 256 blocks of one device, at most 4 name any one owner device, a bound that some block reaches.
All inputs are finite; a program needn't handle non-finite values.
Results may differ from the reference program's by a relative error of at most 0.0003.
Values sent between devices are 32-bit elements; how exact they have to be, the bound alone decides.
A program may use at most 64 MiB of HBM per device.

```python
import math
import jax
import jax.numpy as jnp
import numpy as np
from jax import lax

TB = 128
F = 3
K = 4
NB_B = 64
MB = 8
BA = 256
CAP = 4
NW = 80
A_BLOCKS = 32768
A_ROWS = 4194304
B_ROWS = 1048576
N_ZONE = 16
N_TILE = 8
DEVICES = 128


def with_ends(values, key, smallest, top_value):
    place = [jax.random.randint(jax.random.fold_in(key, axis), (), 0, length) for axis, length in enumerate(values.shape)]
    longest = values.shape.index(max(values.shape))
    neighbour = place[:longest] + [(place[longest] + 1) % values.shape[longest]] + place[longest + 1:]
    return values.at[tuple(place)].set(smallest).at[tuple(neighbour)].set(top_value)


def level_of(key, dims, cuts, smallest, high):
    def one(dim, shards_of):
        steps = jax.random.uniform(jax.random.fold_in(jax.random.fold_in(key, 6), dim), (shards_of,), jnp.float32, smallest / len(cuts), high / len(cuts))
        return jnp.repeat(jnp.exp(steps), dims[dim] // shards_of).reshape((-1,) + (1,) * (len(dims) - dim - 1))

    gain = one(*cuts[0])
    for cut in cuts[1:]:
        gain = gain * one(*cut)
    return gain


def deal_out(stream_key, own, number, rows, count, top, limit, slope):
    sequence = jax.random.permutation(stream_key, count)
    heavy_load, common = load_shares(count, rows * top, limit, slope, True), load_shares(count, rows * top, limit, slope, False)
    places = jnp.arange(count)

    def named(lengths, turn):
        used = int((lengths > 0).sum())
        fixed = max(1, used // 4)
        moved = fixed + (places - fixed + turn * (used - fixed)) % max(1, count - fixed)
        return jnp.zeros((count,), jnp.int32).at[sequence[jnp.where(places < fixed, places, moved)]].set(jnp.asarray(lengths, jnp.int32))

    lengths = jnp.where(number % 4 == 0, named(heavy_load, number // 4), named(common, number - number // 4 - 1))
    mixed = jax.random.permutation(jax.random.fold_in(own, 3), count)
    donor, taker = mixed[0:count // 2 * 2:2], mixed[1:count // 2 * 2:2]
    room = jnp.minimum(lengths[donor] - 1, limit - lengths[taker]) // 2
    room = jnp.where((donor == sequence[0]) | (taker == sequence[0]) | (lengths[taker] == 0), 0, jnp.maximum(room, 0))
    moved = jax.random.randint(jax.random.fold_in(own, 4), (count // 2,), 0, 1 << 20) % (room + 1)
    lengths = lengths.at[donor].add(-moved).at[taker].add(moved)
    members = jnp.searchsorted(jnp.cumsum(lengths), jnp.arange(rows * top), side="right").astype(jnp.int32)
    table = members.reshape(top, rows).T
    table = table[jax.random.permutation(jax.random.fold_in(own, 1), rows)]
    turn = jax.random.randint(jax.random.fold_in(own, 2), (rows, 1), 0, top)
    return jnp.take_along_axis(table, (jnp.arange(top)[None, :] + turn) % top, axis=1)


def load_shares(count, total, most, lean, full):
    portions = [(1 << 20) // math.isqrt(grade ** lean) + 1 for grade in range(1, count + 1)]
    largest = most if full else min(most, max(-(-total // count), total * portions[0] // sum(portions)))
    least = 1 if total - largest >= count - 1 else 0
    holding, spare = [largest] + [least] * (count - 1), total - largest - least * (count - 1)
    while spare > 0:
        free = [i for i in range(1, count) if holding[i] < largest] or [i for i in range(1, count) if holding[i] < most]
        whole, budget = sum([portions[i] for i in free]), spare
        for i in free:
            more = min(most - holding[i], max(1, budget * portions[i] // whole), spare)
            holding[i] = holding[i] + more
            spare = spare - more
    return np.array(holding)


def centred(key, extent, scale, reach, cuts=(), kind=jnp.bfloat16):
    array = scale * jax.random.normal(key, extent, jnp.float32)
    if cuts:
        array = array * level_of(key, extent, cuts, -0.22, 0.18)
    return jnp.clip(array, -reach, reach).astype(kind)


def setup_inputs(seed: int = 0) -> dict:
    splits = jax.random.split(jax.random.key(seed), 10)
    a_coord = centred(splits[0], (2, A_ROWS), 1.0, 6.0, ((1, 128),), jnp.float32)
    a_var = jnp.clip(jnp.exp(math.log(1.0) - 2.3025851 * jax.random.uniform(splits[1], (A_ROWS,), jnp.float32) ** level_of(splits[1], (A_ROWS,), ((0, 128),), -0.2, 0.2)), 0.1, 1.0)
    dest_keys = jax.random.split(jax.random.fold_in(splits[2], 1), A_BLOCKS // BA)
    dest_turns = jax.random.permutation(jax.random.fold_in(splits[2], 3), A_BLOCKS // BA)
    dest = jax.vmap(lambda own, number: deal_out(jax.random.fold_in(splits[2], 2), own, number, BA, DEVICES, 1, CAP, 2))(dest_keys, dest_turns).reshape((A_BLOCKS, 1))
    cand = with_ends(jax.random.randint(splits[3], (A_BLOCKS, K), 0, NW), jax.random.fold_in(splits[3], 1), 0, NW - 1).astype(jnp.int32)
    cand_count = with_ends(jax.random.randint(splits[4], (A_BLOCKS, 1), 1, K + 1), jax.random.fold_in(splits[4], 1), 1, K).astype(jnp.int32)
    b_coord = centred(splits[5], (2, B_ROWS), 1.0, 6.0, ((1, 128),), jnp.float32)
    b_var = jnp.clip(jnp.exp(math.log(1.0) - 2.3025851 * jax.random.uniform(splits[6], (B_ROWS,), jnp.float32) ** level_of(splits[6], (B_ROWS,), ((0, 128),), -0.2, 0.2)), 0.1, 1.0)
    b_prior = jnp.clip(jnp.exp(math.log(0.02) - 2.30258502 * jax.random.uniform(splits[7], (B_ROWS,), jnp.float32) ** level_of(splits[7], (B_ROWS,), ((0, 128),), -0.2, 0.2)), 0.002, 0.02)
    b_flux = centred(splits[8], (F, B_ROWS), 1.0, 6.0, ((1, 128),), jnp.float32)
    return dict(a_coord=a_coord, a_var=a_var, dest=dest, cand=cand, cand_count=cand_count, b_coord=b_coord, b_var=b_var, b_prior=b_prior, b_flux=b_flux)


def slot_match(a_block, candidates, live_count):
    numerator = jnp.zeros((5, a_block.shape[1]), jnp.float32)
    weight_sum = jnp.zeros((a_block.shape[1],), jnp.float32)
    for position in range(len(candidates)):
        block_data = candidates[position]
        is_live = jnp.where(live_count > position, 1.0, 0.0).astype(jnp.float32)
        delta_u = a_block[0][:, None] - block_data[0][None, :]
        delta_v = a_block[1][:, None] - block_data[1][None, :]
        var_sum = a_block[2][:, None] + block_data[5][None, :]
        weight = (block_data[6] * is_live)[None, :] * (2.0 / var_sum) * jnp.exp(-(delta_u * delta_u + delta_v * delta_v) / (2.0 * var_sum))
        numerator = numerator + jnp.einsum("fj,ij->fi", block_data[:5], weight, precision=lax.Precision.HIGHEST)
        weight_sum = weight_sum + jnp.sum(weight, axis=1)
    inverse = 1.0 / (1.0 + weight_sum)
    return jnp.concatenate([numerator * inverse[None, :], (weight_sum * inverse)[None, :]], axis=0)


def reference(a_coord, a_var, dest, cand, cand_count, b_coord, b_var, b_prior, b_flux):
    devices = N_ZONE * N_TILE
    b_stack = jnp.concatenate([b_coord, b_flux, b_var[None, :], b_prior[None, :]], axis=0)
    b_blocks = b_stack.reshape(7, devices * NB_B, TB).transpose(1, 0, 2)
    a_stack = jnp.concatenate([a_coord, a_var[None, :]], axis=0)
    a_blocks = a_stack.reshape(3, A_BLOCKS, TB).transpose(1, 0, 2)

    def match_block(items):
        a_block, target, names, live_count = items
        zone_row = target // N_TILE
        candidates = []
        for position in range(K):
            window_pos = names[position]
            lower_block = (target - N_TILE) * NB_B + NB_B - MB + window_pos
            own_block = target * NB_B + window_pos - MB
            upper_block = (target + N_TILE) * NB_B + window_pos - MB - NB_B
            chosen = jnp.where(window_pos < MB, lower_block, jnp.where(window_pos < MB + NB_B, own_block, upper_block))
            valid = jnp.where(window_pos < MB, zone_row > 0, jnp.where(window_pos < MB + NB_B, True, zone_row < N_ZONE - 1))
            chosen = jnp.clip(chosen, 0, devices * NB_B - 1).astype(jnp.int32)
            candidates.append(b_blocks[chosen] * valid.astype(jnp.float32))
        return slot_match(a_block, candidates, live_count)

    results = lax.map(match_block, (a_blocks, dest[:, 0], cand, cand_count[:, 0]), batch_size=256)
    results = results.transpose(1, 0, 2).reshape(6, A_ROWS)
    return results[:5], results[5]
```

```python
import functools
import math

import jax
import jax.numpy as jnp
from jax import lax
from jax.experimental import pallas as pl
from jax.experimental.pallas import tpu as pltpu
from jax.sharding import PartitionSpec as P

TB = 128
K = 4
MB = 8
CAP = 4
UNROLL = 16
SCALE = math.sqrt(0.5 / math.log(2.0))
F32 = jnp.float32
BF16 = jnp.bfloat16


def pack_kernel(dest, a_coord, a_var, labels, send, place, taken):
    devices = taken.shape[0]
    send[...] = jnp.zeros_like(send)

    def clear(i, c):
        taken[i] = 0
        return c

    lax.fori_loop(0, devices, clear, 0, unroll=8)

    def one(b, c):
        d = dest[b]
        r = taken[d]
        taken[d] = r + 1
        place[b] = d * 4 + r
        row = d * 16 + r
        lanes = pl.ds(pl.multiple_of(b * TB, TB), TB)
        send[pl.ds(row, 1), :] = a_coord[0:1, lanes]
        send[pl.ds(row + 4, 1), :] = a_coord[1:2, lanes]
        send[pl.ds(row + 8, 1), :] = a_var[pl.ds(b, 1), :]
        send[pl.ds(row + 12, 1), :] = labels[pl.ds(b, 1), :]
        return c

    lax.fori_loop(0, dest.shape[0], one, 0, unroll=4)


def match_kernel(labels, a_rows, window, out, wide, acc, todo):
    slots = a_rows.shape[0] // 4
    messages = slots // CAP
    blocks = window.shape[1] // TB
    steps = 16
    row = lax.broadcasted_iota(jnp.int32, (8, TB), 0)
    acc[...] = jnp.zeros_like(acc)

    def prepare(step, n):
        for k in range(blocks // steps):
            w = step * (blocks // steps) + k
            tile = window[:, pl.ds(pl.multiple_of(w * TB, TB), TB)]
            for q, line, gain in ((0, 0, SCALE), (1, 1, SCALE), (2, 5, 1.0)):
                wide[w, q] = jnp.broadcast_to(tile[line : line + 1] * gain, (TB, TB)).T
        for k in range(messages // steps * CAP):
            slot = step * (messages // steps * CAP) + k
            for p in range(K):
                todo[n + p] = slot * TB + labels[slot * 5 + p]
            n = n + labels[slot * 5 + K]
        return n

    pairs = lax.fori_loop(0, steps, prepare, 0)
    for k in range(UNROLL):
        todo[pairs + k] = slots * TB

    def pair(code):
        slot = jnp.minimum(code // TB, slots - 1)
        w = code % TB
        base = slot // CAP * 16 + slot % CAP
        tile = window[:, pl.ds(pl.multiple_of(w * TB, TB), TB)]
        du = wide[w, 0] - a_rows[pl.ds(base, 1), :] * SCALE
        dv = wide[w, 1] - a_rows[pl.ds(base + 4, 1), :] * SCALE
        r = pltpu.reciprocal(wide[w, 2] + a_rows[pl.ds(base + 8, 1), :], approx=True)
        weight = r * jnp.exp2((du * du + dv * dv) * -r)
        q = jnp.where(row == 5, 2.0, 2.0 * tile) * tile[6:7]
        q_high = q.astype(BF16).astype(F32)
        q = jnp.concatenate([q_high, q - q_high], axis=0).astype(BF16)
        high = weight.astype(BF16)
        low = (weight - high.astype(F32)).astype(BF16)
        total = jnp.dot(
            jnp.concatenate([q, q], axis=1),
            jnp.concatenate([high, low], axis=0),
            preferred_element_type=F32,
        )
        return total[0:8] + total[8:16]

    def chunk(c, carry):
        done = []
        for k in range(UNROLL):
            code = todo[c * UNROLL + k]
            done.append((code // TB, pair(code)))
        for slot, total in done:
            acc[slot] = acc[slot] + total
        return carry

    lax.fori_loop(0, (pairs + UNROLL - 1) // UNROLL, chunk, 0)

    def finish(m, carry):
        parts = []
        for r in range(CAP):
            total = acc[m * CAP + r]
            parts.append((total / (1.0 + total[5:6]))[0:6])
        out[m] = jnp.concatenate(parts, axis=0)
        return carry

    lax.fori_loop(0, messages, finish, 0, unroll=2)


def unpack_kernel(place, back, matched, prob):
    def one(b, c):
        slot = place[b]
        base = slot // CAP * 24 + slot % CAP * 6
        lanes = pl.ds(pl.multiple_of(b * TB, TB), TB)
        for q in range(5):
            matched[q : q + 1, lanes] = back[pl.ds(base + q, 1), :]
        prob[pl.ds(b, 1), :] = back[pl.ds(base + 5, 1), :]
        return c

    lax.fori_loop(0, place.shape[0], one, 0, unroll=4)


VMEM = pl.BlockSpec(memory_space=pltpu.VMEM)
SMEM = pl.BlockSpec(memory_space=pltpu.SMEM)


def params(mib):
    return pltpu.CompilerParams(vmem_limit_bytes=mib * 2**20)


def body(a_coord, a_var, dest, cand, cand_count, b_coord, b_var, b_prior, b_flux):
    zones = lax.axis_size("zone")
    devices = zones * lax.axis_size("tile")
    count = dest.shape[0]
    labels = jnp.concatenate([cand, cand_count], axis=1).astype(F32)
    labels = jnp.pad(labels, ((0, 0), (0, TB - K - 1)))
    send, place = pl.pallas_call(
        pack_kernel,
        out_shape=(
            jax.ShapeDtypeStruct((devices * 16, TB), F32),
            jax.ShapeDtypeStruct((count,), jnp.int32),
        ),
        in_specs=[SMEM, VMEM, VMEM, VMEM],
        out_specs=(VMEM, SMEM),
        scratch_shapes=[pltpu.SMEM((devices,), jnp.int32)],
        compiler_params=params(16),
        name="pack",
    )(dest.reshape(count), a_coord, a_var.reshape(count, TB), labels)
    got = lax.all_to_all(
        send.reshape(devices, 16, TB), ("zone", "tile"), split_axis=0, concat_axis=0, tiled=True
    )
    own = jnp.concatenate(
        [b_coord, b_flux, b_var[None, :], b_prior[None, :], jnp.zeros_like(b_var)[None, :]], axis=0
    )
    width = MB * TB
    up = [(i, i + 1) for i in range(zones - 1)]
    below = lax.ppermute(own[:, -width:], "zone", up)
    above = lax.ppermute(own[:, :width], "zone", [(j, i) for i, j in up])
    window = jnp.concatenate([below, own, above], axis=1)
    got_labels = got[:, 12:16, : K + 1].astype(jnp.int32).reshape(-1)
    slots = devices * CAP
    result = pl.pallas_call(
        match_kernel,
        out_shape=jax.ShapeDtypeStruct((devices, CAP * 6, TB), F32),
        in_specs=[SMEM, VMEM, VMEM],
        out_specs=VMEM,
        scratch_shapes=[
            pltpu.VMEM((window.shape[1] // TB, 3, TB, TB), F32),
            pltpu.VMEM((slots + 1, 8, TB), F32),
            pltpu.SMEM((slots * K + UNROLL + K,), jnp.int32),
        ],
        compiler_params=params(40),
        name="match",
    )(got_labels, got.reshape(devices * 16, TB), window)
    back = lax.all_to_all(result, ("zone", "tile"), split_axis=0, concat_axis=0, tiled=True)
    matched, prob = pl.pallas_call(
        unpack_kernel,
        out_shape=(
            jax.ShapeDtypeStruct((5, count * TB), F32),
            jax.ShapeDtypeStruct((count, TB), F32),
        ),
        in_specs=[SMEM, VMEM],
        out_specs=(VMEM, VMEM),
        compiler_params=params(16),
        name="unpack",
    )(place, back.reshape(slots * 6, TB))
    return matched, prob.reshape(count * TB)


def solution(mesh):
    both = ("zone", "tile")
    rows, columns, flat = P(both, None), P(None, both), P(both)
    return jax.shard_map(
        body,
        mesh=mesh,
        in_specs=(columns, flat, rows, rows, rows, columns, flat, flat, columns),
        out_specs=(columns, flat),
        check_vma=False,
    )
```

```python
import functools
import math

import jax
import jax.numpy as jnp
from jax import lax
from jax.experimental import pallas as pl
from jax.experimental.pallas import tpu as pltpu
from jax.sharding import PartitionSpec as P

TB = 128
K = 4
MB = 8
CAP = 4
UNROLL = 20
GROUP = 2
TERMS = 24
DEAD = 127
SCALE = math.sqrt(0.5 / math.log(2.0))
F32 = jnp.float32
BF16 = jnp.bfloat16


def pack_kernel(dest, a_coord, a_var, labels, send, place, taken):
    devices = taken.shape[0]
    send[...] = jnp.zeros_like(send)

    def clear(i, c):
        taken[i] = 0
        return c

    lax.fori_loop(0, devices, clear, 0, unroll=8)

    def one(b, c):
        d = dest[b]
        r = taken[d]
        taken[d] = r + 1
        place[b] = d * 4 + r
        row = d * 16 + r
        lanes = pl.ds(pl.multiple_of(b * TB, TB), TB)
        send[pl.ds(row, 1), :] = a_coord[0:1, lanes]
        send[pl.ds(row + 4, 1), :] = a_coord[1:2, lanes]
        send[pl.ds(row + 8, 1), :] = a_var[pl.ds(b, 1), :]
        send[pl.ds(row + 12, 1), :] = labels[pl.ds(b, 1), :]
        return c

    lax.fori_loop(0, dest.shape[0], one, 0, unroll=4)


def split(x):
    first = x.astype(BF16).astype(F32)
    second = (x - first).astype(BF16).astype(F32)
    return first, second, x - first - second


def left_terms(tile):
    u, v = tile[0:1] * SCALE, tile[1:2] * SCALE
    u, v, n = split(u), split(v), split(u * u + v * v)
    one = jnp.ones_like(u[0])
    rows = [u[0], v[0], u[0], v[0], u[0], v[0], one, one]
    rows += [u[1], v[1], u[1], v[1], u[2], v[2], one, n[0], n[1], n[2]]
    return jnp.concatenate(rows + [jnp.zeros((TB - len(rows), TB), F32)], axis=0)


def right_terms(a_rows, right, g):
    for r in range(CAP):
        u, v = (a_rows[pl.ds(g * 128 + 4 * q + r, 8, stride=16), :] * SCALE for q in range(2))
        n = split(u * u + v * v)
        u, v = split(-2.0 * u), split(-2.0 * v)
        one = jnp.ones_like(u[0])
        rows = [u[0], v[0], u[1], v[1], u[2], v[2], n[0], n[1]]
        rows += [u[0], v[0], u[1], v[1], u[0], v[0], n[2], one]
        rows += [one] * (TERMS - len(rows))
        for k, x in enumerate(rows):
            right[pl.ds((g * 8 * CAP + r) * TERMS + k, 8, stride=CAP * TERMS), :] = x


def sort_pairs(a_rows, order, codes):
    messages = a_rows.shape[0] // 16
    line = lax.broadcasted_iota(jnp.int32, (TB, messages), 0).astype(F32)
    lane = lax.broadcasted_iota(jnp.int32, (1, messages), 1)
    keys = [None] * 16
    for r in range(CAP):
        turned = a_rows[pl.ds(12 + r, messages, stride=16), :].T
        for k in range(K):
            keys[4 * k + r] = jnp.where(turned[K : K + 1] > k, turned[k : k + 1], float(DEAD))
    marks = [(line == key).astype(F32) for key in keys]
    here = functools.reduce(jnp.add, marks)
    before = lax.broadcasted_iota(jnp.int32, (TB, TB), 0) < lax.broadcasted_iota(jnp.int32, (TB, TB), 1)
    before = before.astype(F32)
    after = before.T.astype(BF16)
    both = jnp.concatenate([before, jnp.ones_like(before)], axis=1).astype(BF16)
    sums = jnp.dot(here.astype(BF16), both, preferred_element_type=F32)
    groups = jnp.floor((sums[:, TB:] + (GROUP - 1)) * (1.0 / GROUP))
    coarse = jnp.floor(groups * (1.0 / 16))
    first = 16.0 * jnp.dot(after, coarse.astype(BF16), preferred_element_type=F32)
    first = first + jnp.dot(after, (groups - 16.0 * coarse).astype(BF16), preferred_element_type=F32)
    place = sums[:, :TB] + GROUP * first
    for row in range(16):
        spot = jnp.sum(marks[row] * place, axis=0, keepdims=True)
        live = keys[row] < DEAD
        order[row : row + 1, :] = jnp.where(live, spot, float(order_dump(messages))).astype(jnp.int32)
        codes[row : row + 1, :] = (lane * CAP + row % 4) * TB + keys[row].astype(jnp.int32)
        if row < 15:
            place = place + marks[row]
    order[16:17, :] = first[DEAD : DEAD + 1].astype(jnp.int32)


def order_dump(messages):
    return messages * CAP * K + 80 * (GROUP - 1) + GROUP * UNROLL


def list_size(messages):
    return order_dump(messages) + 1


def prepare_kernel(window, wide, left):
    def one(w, c):
        tile = window[:, pl.ds(pl.multiple_of(w * TB, TB), TB)]
        wide[w] = jnp.broadcast_to(-tile[5:6], (TB, TB)).T
        left[w] = left_terms(tile).T.astype(BF16)
        return c

    lax.fori_loop(0, wide.shape[0], one, 0, unroll=4)


def match_kernel(a_rows, window, wide_far, left_far, out, wide, left, right, acc, order, codes, blank, order_s, codes_s, todo, sems):
    messages = a_rows.shape[0] // 16
    slots = messages * CAP
    row = lax.broadcasted_iota(jnp.int32, (8, TB), 0)
    fetches = [
        pltpu.make_async_copy(wide_far, wide, sems.at[3]),
        pltpu.make_async_copy(left_far, left, sems.at[4]),
    ]
    for fetch in fetches:
        fetch.start()
    sort_pairs(a_rows, order, codes)
    blank[...] = jnp.full(blank.shape, slots * TB, jnp.int32)
    copies = [
        pltpu.make_async_copy(order, order_s, sems.at[0]),
        pltpu.make_async_copy(codes, codes_s, sems.at[1]),
        pltpu.make_async_copy(blank, todo, sems.at[2]),
    ]
    for copy in copies:
        copy.start()
    acc[...] = jnp.zeros_like(acc)

    def turn(g, c):
        right_terms(a_rows, right, g)
        return c

    lax.fori_loop(0, messages // 8, turn, 0)
    for copy in copies:
        copy.wait()

    def put(m, c):
        for e in range(16):
            p = order_s[e, m]
            todo[p] = codes_s[e, m]
        return c

    lax.fori_loop(0, messages, put, 0, unroll=2)
    for fetch in fetches:
        fetch.wait()
    groups = order_s[16, 0]

    def group(code):
        w = code[0] & (TB - 1)
        slot = [jnp.minimum(lax.shift_right_logical(c, 7), slots - 1) for c in code]
        base = [lax.shift_right_logical(s, 2) * 16 + (s & 3) for s in slot]
        tile = window[:, pl.ds(pl.multiple_of(w * TB, TB), TB)]

        spare = jnp.zeros((32 - TERMS, TB), F32)
        terms = [
            jnp.concatenate([right[pl.ds(pl.multiple_of(t * TERMS, 8), TERMS), :], spare], axis=0)
            for t in slot
        ]
        terms = jnp.concatenate(terms, axis=1).astype(BF16)
        apart = jnp.dot(left[w][:, :32], terms, preferred_element_type=F32)
        spread = [jnp.broadcast_to(a_rows[pl.ds(b + 8, 1), :], (8, TB)) for b in base]
        high, low = [[] for _ in code], [[] for _ in code]
        for strip in range(0, TB, 16):
            s = [wide[w, strip + h : strip + h + 8, :] for h in (0, 8)]
            for e in range(GROUP):
                weight = []
                for h in range(2):
                    d2 = apart[strip + 8 * h : strip + 8 * h + 8, e * TB : (e + 1) * TB]
                    r = pltpu.reciprocal(s[h] - spread[e], approx=True)
                    weight.append(r * jnp.exp2(d2 * r))
                weight = jnp.concatenate(weight, axis=0)
                high[e].append(weight.astype(BF16))
                low[e].append((weight - high[e][-1].astype(F32)).astype(BF16))
        q = jnp.where(row == 5, -2.0, -2.0 * tile) * tile[6:7]
        q_high = q.astype(BF16).astype(F32)
        q = jnp.concatenate([q_high, q - q_high], axis=0).astype(BF16)
        q = jnp.concatenate([q, q], axis=1)
        total = []
        for e in range(GROUP):
            t = jnp.dot(q, jnp.concatenate(high[e] + low[e], axis=0), preferred_element_type=F32)
            total.append(t[0:8] + t[8:16])
        return total

    def chunk(c, carry):
        done = []
        for k in range(UNROLL):
            code = [todo[(c * UNROLL + k) * GROUP + e] for e in range(GROUP)]
            done.append((code, group(code)))
        for code, total in done:
            for e in range(GROUP):
                slot = lax.shift_right_logical(code[e], 7)
                acc[slot] = acc[slot] + total[e]
        return carry

    lax.fori_loop(0, (groups + UNROLL - 1) // UNROLL, chunk, 0)

    def finish(m, carry):
        parts = []
        for r in range(CAP):
            total = acc[m * CAP + r]
            parts.append((total / (1.0 + total[5:6]))[0:6])
        out[m] = jnp.concatenate(parts, axis=0)
        return carry

    lax.fori_loop(0, messages, finish, 0, unroll=2)


def unpack_kernel(place, back, matched, prob):
    def one(b, c):
        slot = place[b]
        base = slot // CAP * 24 + slot % CAP * 6
        lanes = pl.ds(pl.multiple_of(b * TB, TB), TB)
        for q in range(5):
            matched[q : q + 1, lanes] = back[pl.ds(base + q, 1), :]
        prob[pl.ds(b, 1), :] = back[pl.ds(base + 5, 1), :]
        return c

    lax.fori_loop(0, place.shape[0], one, 0, unroll=4)


VMEM = pl.BlockSpec(memory_space=pltpu.VMEM)
FAR = pl.BlockSpec(memory_space=pl.ANY)
SMEM = pl.BlockSpec(memory_space=pltpu.SMEM)


def params(mib):
    return pltpu.CompilerParams(vmem_limit_bytes=mib * 2**20)


def prepare_call(window):
    blocks = window.shape[1] // TB
    return pl.pallas_call(
        prepare_kernel,
        out_shape=(
            jax.ShapeDtypeStruct((blocks, TB, TB), F32),
            jax.ShapeDtypeStruct((blocks, TB, TB), BF16),
        ),
        in_specs=[VMEM],
        out_specs=(VMEM, VMEM),
        compiler_params=params(16),
        cost_estimate=pl.CostEstimate(flops=10**8, bytes_accessed=10**7, transcendentals=0),
        name="prepare",
    )(window)


def match_call(a_rows, window, wide, left):
    messages = a_rows.shape[0] // 16
    size = -(-list_size(messages) // 1024) * 1024
    return pl.pallas_call(
        match_kernel,
        out_shape=jax.ShapeDtypeStruct((messages, CAP * 6, TB), F32),
        in_specs=[VMEM, VMEM, FAR, FAR],
        out_specs=VMEM,
        scratch_shapes=[
            pltpu.VMEM(wide.shape, wide.dtype),
            pltpu.VMEM(left.shape, left.dtype),
            pltpu.VMEM((messages * CAP * TERMS, TB), F32),
            pltpu.VMEM((messages * CAP + 1, 8, TB), F32),
            pltpu.VMEM((24, messages), jnp.int32),
            pltpu.VMEM((16, messages), jnp.int32),
            pltpu.VMEM((size,), jnp.int32),
            pltpu.SMEM((24, messages), jnp.int32),
            pltpu.SMEM((16, messages), jnp.int32),
            pltpu.SMEM((size,), jnp.int32),
            pltpu.SemaphoreType.DMA((5,)),
        ],
        compiler_params=params(28),
        name="match",
    )(a_rows, window, wide, left)


def body(a_coord, a_var, dest, cand, cand_count, b_coord, b_var, b_prior, b_flux):
    zones = lax.axis_size("zone")
    devices = zones * lax.axis_size("tile")
    count = dest.shape[0]
    labels = jnp.concatenate([cand, cand_count], axis=1).astype(F32)
    labels = jnp.pad(labels, ((0, 0), (0, TB - K - 1)))
    send, place = pl.pallas_call(
        pack_kernel,
        out_shape=(
            jax.ShapeDtypeStruct((devices * 16, TB), F32),
            jax.ShapeDtypeStruct((count,), jnp.int32),
        ),
        in_specs=[SMEM, VMEM, VMEM, VMEM],
        out_specs=(VMEM, SMEM),
        scratch_shapes=[pltpu.SMEM((devices,), jnp.int32)],
        compiler_params=params(16),
        name="pack",
    )(dest.reshape(count), a_coord, a_var.reshape(count, TB), labels)
    send, b_coord, b_flux, b_var, b_prior = lax.optimization_barrier(
        (send, b_coord, b_flux, b_var, b_prior)
    )
    got = lax.all_to_all(
        send.reshape(devices, 16, TB), ("zone", "tile"), split_axis=0, concat_axis=0, tiled=True
    )
    own = jnp.concatenate(
        [b_coord, b_flux, b_var[None, :], b_prior[None, :], jnp.zeros_like(b_var)[None, :]], axis=0
    )
    width = MB * TB
    up = [(i, i + 1) for i in range(zones - 1)]
    below = lax.ppermute(own[:, -width:], "zone", up)
    above = lax.ppermute(own[:, :width], "zone", [(j, i) for i, j in up])
    window = jnp.concatenate([below, own, above], axis=1)
    slots = devices * CAP
    result = match_call(got.reshape(devices * 16, TB), window, *prepare_call(window))
    back = lax.all_to_all(result, ("zone", "tile"), split_axis=0, concat_axis=0, tiled=True)
    matched, prob = pl.pallas_call(
        unpack_kernel,
        out_shape=(
            jax.ShapeDtypeStruct((5, count * TB), F32),
            jax.ShapeDtypeStruct((count, TB), F32),
        ),
        in_specs=[SMEM, VMEM],
        out_specs=(VMEM, VMEM),
        compiler_params=params(16),
        name="unpack",
    )(place, back.reshape(slots * 6, TB))
    return matched, prob.reshape(count * TB)


def solution(mesh):
    both = ("zone", "tile")
    rows, columns, flat = P(both, None), P(None, both), P(both)
    return jax.shard_map(
        body,
        mesh=mesh,
        in_specs=(columns, flat, rows, rows, rows, columns, flat, flat, columns),
        out_specs=(columns, flat),
        check_vma=False,
    )
```

```python
import functools
import math

import jax
import jax.numpy as jnp
from jax import lax
from jax.experimental import pallas as pl
from jax.experimental.pallas import tpu as pltpu
from jax.sharding import PartitionSpec as P

TB = 128
K = 4
MB = 8
CAP = 4
UNROLL = 20
GROUP = 2
TERMS = 32
DEAD = 127
SCALE = math.sqrt(0.5 / math.log(2.0))
F32 = jnp.float32
BF16 = jnp.bfloat16


def pack_kernel(dest, far_coord, far_var, labels, send, place, taken, a_coord, a_var, sems):
    devices = taken.shape[0]
    fetches = [
        pltpu.make_async_copy(far_coord, a_coord, sems.at[0]),
        pltpu.make_async_copy(far_var, a_var, sems.at[1]),
    ]
    for fetch in fetches:
        fetch.start()
    send[...] = jnp.zeros_like(send)

    def clear(i, c):
        taken[i] = 0
        return c

    lax.fori_loop(0, devices, clear, 0, unroll=8)
    for fetch in fetches:
        fetch.wait()

    def one(b, c):
        d = dest[b]
        r = taken[d]
        taken[d] = r + 1
        place[b] = d * (CAP * 6) + r * 6
        row = d * 16 + r * 4
        lanes = pl.ds(pl.multiple_of(b * TB, TB), TB)
        send[pl.ds(row, 1), :] = a_coord[0:1, lanes]
        send[pl.ds(row + 1, 1), :] = a_coord[1:2, lanes]
        send[pl.ds(row + 2, 1), :] = a_var[pl.ds(b, 1), :]
        send[pl.ds(row + 3, 1), :] = labels[pl.ds(b, 1), :]
        return c

    lax.fori_loop(0, dest.shape[0], one, 0, unroll=8)


def split(x):
    first = x.astype(BF16).astype(F32)
    second = (x - first).astype(BF16).astype(F32)
    return first, second, x - first - second


def left_terms(tile):
    u, v = tile[0:1] * SCALE, tile[1:2] * SCALE
    u, v, n = split(u), split(v), split(u * u + v * v)
    one = jnp.ones_like(u[0])
    zero = jnp.zeros_like(one)
    rows = [u[0], v[0], one, n[0], u[0], v[0], one, zero, u[0], v[0], one, zero]
    rows += [u[1], v[1], zero, n[1], u[1], v[1], zero, zero, u[2], v[2], zero, n[2]]
    return jnp.concatenate(rows + [jnp.zeros((TB - len(rows), TB), F32)], axis=0)


def right_terms(a_rows, right, m):
    row = lax.broadcasted_iota(jnp.int32, (8, TB), 0)
    upper, kind = row < 4, row & 3
    for half in range(CAP // 2):
        tile = a_rows[pl.ds(pl.multiple_of(m * 16 + 8 * half, 8), 8), :] * SCALE
        square = tile * tile
        square = pltpu.roll(square, 1, 0) + pltpu.roll(square, 2, 0)
        y = split(jnp.where(kind < 2, -2.0 * tile, jnp.where(kind == 2, square, 1.0)))
        z = [pltpu.roll(x, 4, 0) for x in y]
        for odd in range(2):
            y, z = (z, y) if odd else (y, z)
            parts = [jnp.where(upper, y[i], z[j]) for i, j in ((0, 1), (2, 0), (1, 0))]
            parts = jnp.concatenate(parts + [jnp.zeros((8, TB), F32)], axis=0)
            start = (m * CAP + 2 * half + odd) * TERMS
            right[pl.ds(pl.multiple_of(start, TERMS), TERMS), :] = parts.astype(BF16)


def sort_pairs(a_rows, order, codes):
    messages = a_rows.shape[0] // 16
    line = lax.broadcasted_iota(jnp.int32, (TB, messages), 0).astype(F32)
    lane = lax.broadcasted_iota(jnp.int32, (1, messages), 1)
    keys = [None] * 16
    for r in range(CAP):
        turned = a_rows[pl.ds(4 * r + 3, messages, stride=16), :].T
        for k in range(K):
            keys[4 * k + r] = jnp.where(turned[K : K + 1] > k, turned[k : k + 1], float(DEAD))
    marks = [(line == key).astype(F32) for key in keys]
    here = functools.reduce(jnp.add, marks)
    before = lax.broadcasted_iota(jnp.int32, (TB, TB), 0) < lax.broadcasted_iota(jnp.int32, (TB, TB), 1)
    before = before.astype(F32)
    after = before.T.astype(BF16)
    both = jnp.concatenate([before, jnp.ones_like(before)], axis=1).astype(BF16)
    sums = jnp.dot(here.astype(BF16), both, preferred_element_type=F32)
    groups = jnp.floor((sums[:, TB:] + (GROUP - 1)) * (1.0 / GROUP))
    coarse = jnp.floor(groups * (1.0 / 16))
    first = 16.0 * jnp.dot(after, coarse.astype(BF16), preferred_element_type=F32)
    first = first + jnp.dot(after, (groups - 16.0 * coarse).astype(BF16), preferred_element_type=F32)
    place = sums[:, :TB] + GROUP * first
    for row in range(16):
        spot = jnp.sum(marks[row] * place, axis=0, keepdims=True)
        live = keys[row] < DEAD
        order[row : row + 1, :] = jnp.where(live, spot, float(order_dump(messages))).astype(jnp.int32)
        codes[row : row + 1, :] = (lane * CAP + row % 4) * TB + keys[row].astype(jnp.int32)
        if row < 15:
            place = place + marks[row]
    order[16:17, :] = first[DEAD : DEAD + 1].astype(jnp.int32)


def order_dump(messages):
    return messages * CAP * K + 80 * (GROUP - 1) + GROUP * UNROLL


def list_size(messages):
    return order_dump(messages) + 1


def prepare_kernel(window, wide, left):
    def one(w, c):
        tile = window[:, pl.ds(pl.multiple_of(w * TB, TB), TB)]
        wide[w] = jnp.broadcast_to(-tile[5:6], (TB, TB)).T
        left[w] = left_terms(tile).T.astype(BF16)
        return c

    lax.fori_loop(0, wide.shape[0], one, 0, unroll=4)


def match_kernel(
    a_rows, own, below, above, wide_own, left_own, wide_edge, left_edge,
    out, window, wide, left, right, acc, order, codes, blank, order_s, codes_s, todo, sems,
):
    messages = a_rows.shape[0] // 16
    slots = messages * CAP
    blocks = own.shape[1] // TB
    row = lax.broadcasted_iota(jnp.int32, (8, TB), 0)
    fetches = []
    for edge, inner, there in ((wide_edge, wide_own, wide), (left_edge, left_own, left)):
        fetches.append((edge.at[0:MB], there.at[0:MB]))
        fetches.append((inner, there.at[MB : MB + blocks]))
        fetches.append((edge.at[MB : 2 * MB], there.at[MB + blocks : 2 * MB + blocks]))
    fetches.append((below, window.at[:, 0 : MB * TB]))
    fetches.append((own, window.at[:, MB * TB : (MB + blocks) * TB]))
    fetches.append((above, window.at[:, (MB + blocks) * TB : (2 * MB + blocks) * TB]))
    fetches = [pltpu.make_async_copy(a, b, sems.at[3 + i]) for i, (a, b) in enumerate(fetches)]
    for fetch in fetches:
        fetch.start()
    sort_pairs(a_rows, order, codes)
    blank[...] = jnp.full(blank.shape, slots * TB, jnp.int32)
    copies = [
        pltpu.make_async_copy(order, order_s, sems.at[0]),
        pltpu.make_async_copy(codes, codes_s, sems.at[1]),
        pltpu.make_async_copy(blank, todo, sems.at[2]),
    ]
    for copy in copies:
        copy.start()
    acc[...] = jnp.zeros_like(acc)

    for copy in copies:
        copy.wait()

    def arrange(g, c):
        for i in range(8):
            m = g * 8 + i
            for e in range(16):
                todo[order_s[e, m]] = codes_s[e, m]
            right_terms(a_rows, right, m)
        return c

    lax.fori_loop(0, messages // 8, arrange, 0)
    for fetch in fetches:
        fetch.wait()
    groups = order_s[16, 0]

    def group(code):
        w = code[0] & (TB - 1)
        slot = [jnp.minimum(lax.shift_right_logical(c, 7), slots - 1) for c in code]
        tile = window[:, pl.ds(pl.multiple_of(w * TB, TB), TB)]

        terms = [right[pl.ds(pl.multiple_of(t * TERMS, TERMS), TERMS), :] for t in slot]
        terms = jnp.concatenate(terms, axis=1)
        apart = jnp.dot(left[w][:, :TERMS], terms, preferred_element_type=F32)
        spread = [jnp.broadcast_to(a_rows[pl.ds(4 * t + 2, 1), :], (8, TB)) for t in slot]
        high, low = [[] for _ in code], [[] for _ in code]
        for strip in range(0, TB, 16):
            s = [wide[w, strip + h : strip + h + 8, :] for h in (0, 8)]
            for e in range(GROUP):
                weight = []
                for h in range(2):
                    d2 = apart[strip + 8 * h : strip + 8 * h + 8, e * TB : (e + 1) * TB]
                    r = pltpu.reciprocal(s[h] - spread[e], approx=True)
                    weight.append(r * jnp.exp2(d2 * r))
                weight = jnp.concatenate(weight, axis=0)
                high[e].append(weight.astype(BF16))
                low[e].append((weight - high[e][-1].astype(F32)).astype(BF16))
        q = jnp.where(row == 5, -2.0, -2.0 * tile) * tile[6:7]
        q_high = q.astype(BF16).astype(F32)
        q = jnp.concatenate([q_high, q - q_high], axis=0).astype(BF16)
        q = jnp.concatenate([q, q], axis=1)
        total = []
        for e in range(GROUP):
            t = jnp.dot(q, jnp.concatenate(high[e] + low[e], axis=0), preferred_element_type=F32)
            total.append(t[0:8] + t[8:16])
        return total

    def chunk(c, carry):
        done = []
        for k in range(UNROLL):
            code = [todo[(c * UNROLL + k) * GROUP + e] for e in range(GROUP)]
            done.append((code, group(code)))
        for code, total in done:
            for e in range(GROUP):
                slot = lax.shift_right_logical(code[e], 7)
                acc[slot] = acc[slot] + total[e]
        return carry

    lax.fori_loop(0, (groups + UNROLL - 1) // UNROLL, chunk, 0)

    def finish(m, carry):
        parts = []
        for r in range(CAP):
            total = acc[m * CAP + r]
            parts.append((total / (1.0 + total[5:6]))[0:6])
        out[m] = jnp.concatenate(parts, axis=0)
        return carry

    lax.fori_loop(0, messages, finish, 0, unroll=2)


def unpack_kernel(place, back, matched, prob):
    def one(b, c):
        base = place[b]
        lanes = pl.ds(pl.multiple_of(b * TB, TB), TB)
        for q in range(5):
            matched[q : q + 1, lanes] = back[pl.ds(base + q, 1), :]
        prob[pl.ds(b, 1), :] = back[pl.ds(base + 5, 1), :]
        return c

    lax.fori_loop(0, place.shape[0], one, 0, unroll=8)


VMEM = pl.BlockSpec(memory_space=pltpu.VMEM)
FAR = pl.BlockSpec(memory_space=pltpu.HBM)
SMEM = pl.BlockSpec(memory_space=pltpu.SMEM)


def params(mib):
    return pltpu.CompilerParams(vmem_limit_bytes=mib * 2**20)


def far(*arrays):
    return [pltpu.with_memory_space_constraint(x, pltpu.HBM) for x in arrays]


def prepare_call(window):
    blocks = window.shape[1] // TB
    return pl.pallas_call(
        prepare_kernel,
        out_shape=(
            jax.ShapeDtypeStruct((blocks, TB, TB), F32),
            jax.ShapeDtypeStruct((blocks, TB, TB), BF16),
        ),
        in_specs=[VMEM],
        out_specs=(VMEM, VMEM),
        compiler_params=params(16),
        cost_estimate=pl.CostEstimate(flops=10**8, bytes_accessed=10**7, transcendentals=0),
        name="prepare",
    )(window)


def match_call(a_rows, own, below, above, *prepared):
    messages = a_rows.shape[0] // 16
    blocks = own.shape[1] // TB + 2 * MB
    size = -(-list_size(messages) // 1024) * 1024
    return pl.pallas_call(
        match_kernel,
        out_shape=jax.ShapeDtypeStruct((messages, CAP * 6, TB), F32),
        in_specs=[VMEM] + [FAR] * 7,
        out_specs=VMEM,
        scratch_shapes=[
            pltpu.VMEM((8, blocks * TB), F32),
            pltpu.VMEM((blocks, TB, TB), F32),
            pltpu.VMEM((blocks, TB, TB), BF16),
            pltpu.VMEM((messages * CAP * TERMS, TB), BF16),
            pltpu.VMEM((messages * CAP + 1, 8, TB), F32),
            pltpu.VMEM((24, messages), jnp.int32),
            pltpu.VMEM((16, messages), jnp.int32),
            pltpu.VMEM((size,), jnp.int32),
            pltpu.SMEM((24, messages), jnp.int32),
            pltpu.SMEM((16, messages), jnp.int32),
            pltpu.SMEM((size,), jnp.int32),
            pltpu.SemaphoreType.DMA((12,)),
        ],
        compiler_params=params(28),
        name="match",
    )(a_rows, *far(own, below, above, *prepared))


def body(a_coord, a_var, dest, cand, cand_count, b_coord, b_var, b_prior, b_flux):
    zones = lax.axis_size("zone")
    devices = zones * lax.axis_size("tile")
    count = dest.shape[0]
    labels = jnp.concatenate([cand, cand_count], axis=1).astype(F32)
    labels = jnp.pad(labels, ((0, 0), (0, TB - K - 1)))
    send, place = pl.pallas_call(
        pack_kernel,
        out_shape=(
            jax.ShapeDtypeStruct((devices * 16, TB), F32),
            jax.ShapeDtypeStruct((count,), jnp.int32),
        ),
        in_specs=[SMEM, FAR, FAR, VMEM],
        out_specs=(VMEM, SMEM),
        scratch_shapes=[
            pltpu.SMEM((devices,), jnp.int32),
            pltpu.VMEM(a_coord.shape, F32),
            pltpu.VMEM((count, TB), F32),
            pltpu.SemaphoreType.DMA((2,)),
        ],
        compiler_params=params(16),
        name="pack",
    )(dest.reshape(count), *far(a_coord, a_var.reshape(count, TB)), labels)
    send, b_coord, b_flux, b_var, b_prior = lax.optimization_barrier(
        (send, b_coord, b_flux, b_var, b_prior)
    )
    got = lax.all_to_all(
        send.reshape(devices, 16, TB), ("zone", "tile"), split_axis=0, concat_axis=0, tiled=True
    )
    own = jnp.concatenate(
        [b_coord, b_flux, b_var[None, :], b_prior[None, :], jnp.zeros_like(b_var)[None, :]], axis=0
    )
    inner = prepare_call(own)
    width = MB * TB
    ends = jnp.concatenate([own[:, -width:], own[:, :width]], axis=1)
    ends, *inner = lax.optimization_barrier((ends, *inner))
    up = [(i, i + 1) for i in range(zones - 1)]
    below = lax.ppermute(ends[:, :width], "zone", up)
    above = lax.ppermute(ends[:, width:], "zone", [(j, i) for i, j in up])
    edge = prepare_call(jnp.concatenate([below, above], axis=1))
    slots = devices * CAP
    result = match_call(got.reshape(devices * 16, TB), own, below, above, *inner, *edge)
    back = lax.all_to_all(result, ("zone", "tile"), split_axis=0, concat_axis=0, tiled=True)
    matched, prob = pl.pallas_call(
        unpack_kernel,
        out_shape=(
            jax.ShapeDtypeStruct((5, count * TB), F32),
            jax.ShapeDtypeStruct((count, TB), F32),
        ),
        in_specs=[SMEM, VMEM],
        out_specs=(VMEM, VMEM),
        compiler_params=params(16),
        name="unpack",
    )(place, back.reshape(slots * 6, TB))
    return matched, prob.reshape(count * TB)


def solution(mesh):
    both = ("zone", "tile")
    rows, columns, flat = P(both, None), P(None, both), P(both)
    return jax.shard_map(
        body,
        mesh=mesh,
        in_specs=(columns, flat, rows, rows, rows, columns, flat, flat, columns),
        out_specs=(columns, flat),
        check_vma=False,
    )
```

```python
import functools
import math

import jax
import jax.numpy as jnp
from jax import lax
from jax.experimental import pallas as pl
from jax.experimental.pallas import tpu as pltpu
from jax.sharding import PartitionSpec as P

TB = 128
K = 4
MB = 8
CAP = 4
UNROLL = 32
GROUP = 2
TERMS = 32
DEAD = 127
SHIFT = 17
SCALE = math.sqrt(0.5 / math.log(2.0))
F32 = jnp.float32
BF16 = jnp.bfloat16


def pack_kernel(dest, far_coord, far_var, labels, send, place, taken, a_coord, a_var, sems):
    devices = taken.shape[0]
    fetches = [
        pltpu.make_async_copy(far_coord, a_coord, sems.at[0]),
        pltpu.make_async_copy(far_var, a_var, sems.at[1]),
    ]
    for fetch in fetches:
        fetch.start()
    send[...] = jnp.zeros_like(send)

    def clear(i, c):
        taken[i] = 0
        return c

    lax.fori_loop(0, devices, clear, 0, unroll=8)
    for fetch in fetches:
        fetch.wait()

    def one(b, c):
        d = dest[b]
        r = taken[d]
        taken[d] = r + 1
        place[b] = d * (CAP * 6) + r * 6
        row = d * 16 + r * 4
        lanes = pl.ds(pl.multiple_of(b * TB, TB), TB)
        send[pl.ds(row, 1), :] = a_coord[0:1, lanes]
        send[pl.ds(row + 1, 1), :] = a_coord[1:2, lanes]
        send[pl.ds(row + 2, 1), :] = a_var[pl.ds(b, 1), :]
        send[pl.ds(row + 3, 1), :] = labels[pl.ds(b, 1), :]
        return c

    lax.fori_loop(0, dest.shape[0], one, 0, unroll=8)


def split(x):
    first = x.astype(BF16).astype(F32)
    second = (x - first).astype(BF16).astype(F32)
    return first, second, x - first - second


def left_terms(tile):
    u, v = tile[0:1] * SCALE, tile[1:2] * SCALE
    u, v, n = split(u), split(v), split(u * u + v * v)
    one = jnp.ones_like(u[0])
    zero = jnp.zeros_like(one)
    rows = [u[0], v[0], one, n[0], u[0], v[0], one, zero, u[0], v[0], one, zero]
    rows += [u[1], v[1], zero, n[1], u[1], v[1], zero, zero, u[2], v[2], zero, n[2]]
    return jnp.concatenate(rows + [jnp.zeros((TB - len(rows), TB), F32)], axis=0)


def right_terms(a_rows, right, m):
    row = lax.broadcasted_iota(jnp.int32, (8, TB), 0)
    upper, kind = row < 4, row & 3
    for half in range(CAP // 2):
        tile = a_rows[pl.ds(pl.multiple_of(m * 16 + 8 * half, 8), 8), :] * SCALE
        square = tile * tile
        square = pltpu.roll(square, 1, 0) + pltpu.roll(square, 2, 0)
        y = split(jnp.where(kind < 2, -2.0 * tile, jnp.where(kind == 2, square, 1.0)))
        z = [pltpu.roll(x, 4, 0) for x in y]
        for odd in range(2):
            y, z = (z, y) if odd else (y, z)
            parts = [jnp.where(upper, y[i], z[j]) for i, j in ((0, 1), (2, 0), (1, 0))]
            parts = jnp.concatenate(parts + [jnp.zeros((8, TB), F32)], axis=0)
            start = (m * CAP + 2 * half + odd) * TERMS
            right[pl.ds(pl.multiple_of(start, TERMS), TERMS), :] = parts.astype(BF16)


def sort_pairs(a_rows, order):
    messages = a_rows.shape[0] // 16
    line = lax.broadcasted_iota(jnp.int32, (TB, messages), 0).astype(F32)
    lane = lax.broadcasted_iota(jnp.int32, (1, messages), 1)
    keys = [None] * 16
    for r in range(CAP):
        turned = a_rows[pl.ds(4 * r + 3, messages, stride=16), :].T
        for k in range(K):
            keys[4 * k + r] = jnp.where(turned[K : K + 1] > k, turned[k : k + 1], float(DEAD))
    marks = [(line == key).astype(F32) for key in keys]
    here = functools.reduce(jnp.add, marks)
    before = lax.broadcasted_iota(jnp.int32, (TB, TB), 0) < lax.broadcasted_iota(jnp.int32, (TB, TB), 1)
    before = before.astype(F32)
    after = before.T.astype(BF16)
    both = jnp.concatenate([before, jnp.ones_like(before)], axis=1).astype(BF16)
    sums = jnp.dot(here.astype(BF16), both, preferred_element_type=F32)
    groups = jnp.floor((sums[:, TB:] + (GROUP - 1)) * (1.0 / GROUP))
    coarse = jnp.floor(groups * (1.0 / 16))
    first = 16.0 * jnp.dot(after, coarse.astype(BF16), preferred_element_type=F32)
    first = first + jnp.dot(after, (groups - 16.0 * coarse).astype(BF16), preferred_element_type=F32)
    place = sums[:, :TB] + GROUP * first
    for row in range(16):
        spot = jnp.sum(marks[row] * place, axis=0, keepdims=True)
        live = keys[row] < DEAD
        spot = jnp.where(live, spot, float(order_dump(messages))).astype(jnp.int32)
        code = (lane * CAP + row % 4) * TB + keys[row].astype(jnp.int32)
        order[row : row + 1, :] = spot * (1 << SHIFT) + code
        if row < 15:
            place = place + marks[row]
    order[16:17, :] = first[DEAD : DEAD + 1].astype(jnp.int32)


def order_dump(messages):
    return messages * CAP * K + 80 * (GROUP - 1) + GROUP * UNROLL


def list_size(messages):
    return order_dump(messages) + 1


def prepare_kernel(window, wide, left):
    def one(w, c):
        tile = window[:, pl.ds(pl.multiple_of(w * TB, TB), TB)]
        wide[w] = jnp.broadcast_to(-tile[5:6], (TB, TB)).T
        left[w] = left_terms(tile).T.astype(BF16)
        return c

    lax.fori_loop(0, wide.shape[0], one, 0, unroll=4)


def match_kernel(
    a_rows, own, below, above, wide_own, left_own, wide_edge, left_edge,
    out, window, wide, left, right, acc, order, blank, order_s, todo, sems,
):
    messages = a_rows.shape[0] // 16
    slots = messages * CAP
    blocks = own.shape[1] // TB
    row = lax.broadcasted_iota(jnp.int32, (8, TB), 0)
    fetches = []
    for edge, inner, there in ((wide_edge, wide_own, wide), (left_edge, left_own, left)):
        fetches.append((edge.at[0:MB], there.at[0:MB]))
        fetches.append((inner, there.at[MB : MB + blocks]))
        fetches.append((edge.at[MB : 2 * MB], there.at[MB + blocks : 2 * MB + blocks]))
    fetches.append((below, window.at[:, 0 : MB * TB]))
    fetches.append((own, window.at[:, MB * TB : (MB + blocks) * TB]))
    fetches.append((above, window.at[:, (MB + blocks) * TB : (2 * MB + blocks) * TB]))
    fetches = [pltpu.make_async_copy(a, b, sems.at[2 + i]) for i, (a, b) in enumerate(fetches)]
    for fetch in fetches:
        fetch.start()
    sort_pairs(a_rows, order)
    blank[...] = jnp.full(blank.shape, slots * TB, jnp.int32)
    copies = [
        pltpu.make_async_copy(order, order_s, sems.at[0]),
        pltpu.make_async_copy(blank, todo, sems.at[1]),
    ]
    for copy in copies:
        copy.start()
    acc[...] = jnp.zeros_like(acc)

    for copy in copies:
        copy.wait()

    def arrange(g, c):
        for m in range(messages):
            word = order_s[g, m]
            todo[lax.shift_right_logical(word, SHIFT)] = word
        for m in range(messages // 16):
            right_terms(a_rows, right, g * (messages // 16) + m)
        return c

    lax.fori_loop(0, 16, arrange, 0)
    for fetch in fetches:
        fetch.wait()
    groups = order_s[16, 0]

    def group(code):
        w = code[0] & (TB - 1)
        slot = [jnp.minimum(lax.shift_right_logical(c, 7), slots - 1) for c in code]
        tile = window[:, pl.ds(pl.multiple_of(w * TB, TB), TB)]

        terms = [right[pl.ds(pl.multiple_of(t * TERMS, TERMS), TERMS), :] for t in slot]
        terms = jnp.concatenate(terms, axis=1)
        apart = jnp.dot(left[w][:, :TERMS], terms, preferred_element_type=F32)
        spread = [jnp.broadcast_to(a_rows[pl.ds(4 * t + 2, 1), :], (8, TB)) for t in slot]
        high, low = [[] for _ in code], [[] for _ in code]
        for strip in range(0, TB, 16):
            s = [wide[w, strip + h : strip + h + 8, :] for h in (0, 8)]
            for e in range(GROUP):
                weight = []
                for h in range(2):
                    d2 = apart[strip + 8 * h : strip + 8 * h + 8, e * TB : (e + 1) * TB]
                    r = pltpu.reciprocal(s[h] - spread[e], approx=True)
                    weight.append(r * jnp.exp2(d2 * r))
                weight = jnp.concatenate(weight, axis=0)
                high[e].append(weight.astype(BF16))
                low[e].append((weight - high[e][-1].astype(F32)).astype(BF16))
        q = jnp.where(row == 5, -2.0, -2.0 * tile) * tile[6:7]
        q_high = q.astype(BF16).astype(F32)
        q = jnp.concatenate([q_high, q - q_high], axis=0).astype(BF16)
        q = jnp.concatenate([q, q], axis=1)
        total = []
        for e in range(GROUP):
            t = jnp.dot(q, jnp.concatenate(high[e] + low[e], axis=0), preferred_element_type=F32)
            total.append(t[0:8] + t[8:16])
        return total

    def chunk(c, carry):
        done = []
        for k in range(UNROLL):
            code = [todo[(c * UNROLL + k) * GROUP + e] & ((1 << SHIFT) - 1) for e in range(GROUP)]
            done.append((code, group(code)))
        for code, total in done:
            for e in range(GROUP):
                slot = lax.shift_right_logical(code[e], 7)
                acc[slot] = acc[slot] + total[e]
        return carry

    lax.fori_loop(0, (groups + UNROLL - 1) // UNROLL, chunk, 0)

    def finish(m, carry):
        parts = []
        for r in range(CAP):
            total = acc[m * CAP + r]
            parts.append((total / (1.0 + total[5:6]))[0:6])
        out[m] = jnp.concatenate(parts, axis=0)
        return carry

    lax.fori_loop(0, messages, finish, 0, unroll=2)


def unpack_kernel(place, back, matched, prob):
    def one(b, c):
        base = place[b]
        lanes = pl.ds(pl.multiple_of(b * TB, TB), TB)
        for q in range(5):
            matched[q : q + 1, lanes] = back[pl.ds(base + q, 1), :]
        prob[pl.ds(b, 1), :] = back[pl.ds(base + 5, 1), :]
        return c

    lax.fori_loop(0, place.shape[0], one, 0, unroll=8)


VMEM = pl.BlockSpec(memory_space=pltpu.VMEM)
FAR = pl.BlockSpec(memory_space=pltpu.HBM)
SMEM = pl.BlockSpec(memory_space=pltpu.SMEM)


def params(mib):
    return pltpu.CompilerParams(vmem_limit_bytes=mib * 2**20)


def far(*arrays):
    return [pltpu.with_memory_space_constraint(x, pltpu.HBM) for x in arrays]


def prepare_call(window):
    blocks = window.shape[1] // TB
    return pl.pallas_call(
        prepare_kernel,
        out_shape=(
            jax.ShapeDtypeStruct((blocks, TB, TB), F32),
            jax.ShapeDtypeStruct((blocks, TB, TB), BF16),
        ),
        in_specs=[VMEM],
        out_specs=(VMEM, VMEM),
        compiler_params=params(16),
        cost_estimate=pl.CostEstimate(flops=10**8, bytes_accessed=10**7, transcendentals=0),
        name="prepare",
    )(window)


def match_call(a_rows, own, below, above, *prepared):
    messages = a_rows.shape[0] // 16
    blocks = own.shape[1] // TB + 2 * MB
    size = -(-list_size(messages) // 1024) * 1024
    return pl.pallas_call(
        match_kernel,
        out_shape=jax.ShapeDtypeStruct((messages, CAP * 6, TB), F32),
        in_specs=[VMEM] + [FAR] * 7,
        out_specs=VMEM,
        scratch_shapes=[
            pltpu.VMEM((8, blocks * TB), F32),
            pltpu.VMEM((blocks, TB, TB), F32),
            pltpu.VMEM((blocks, TB, TB), BF16),
            pltpu.VMEM((messages * CAP * TERMS, TB), BF16),
            pltpu.VMEM((messages * CAP + 1, 8, TB), F32),
            pltpu.VMEM((24, messages), jnp.int32),
            pltpu.VMEM((size,), jnp.int32),
            pltpu.SMEM((24, messages), jnp.int32),
            pltpu.SMEM((size,), jnp.int32),
            pltpu.SemaphoreType.DMA((11,)),
        ],
        compiler_params=params(28),
        name="match",
    )(a_rows, *far(own, below, above, *prepared))


def body(a_coord, a_var, dest, cand, cand_count, b_coord, b_var, b_prior, b_flux):
    zones = lax.axis_size("zone")
    devices = zones * lax.axis_size("tile")
    count = dest.shape[0]
    labels = jnp.concatenate([cand, cand_count], axis=1).astype(F32)
    labels = jnp.pad(labels, ((0, 0), (0, TB - K - 1)))
    send, place = pl.pallas_call(
        pack_kernel,
        out_shape=(
            jax.ShapeDtypeStruct((devices * 16, TB), F32),
            jax.ShapeDtypeStruct((count,), jnp.int32),
        ),
        in_specs=[SMEM, FAR, FAR, VMEM],
        out_specs=(VMEM, SMEM),
        scratch_shapes=[
            pltpu.SMEM((devices,), jnp.int32),
            pltpu.VMEM(a_coord.shape, F32),
            pltpu.VMEM((count, TB), F32),
            pltpu.SemaphoreType.DMA((2,)),
        ],
        compiler_params=params(16),
        name="pack",
    )(dest.reshape(count), *far(a_coord, a_var.reshape(count, TB)), labels)
    send, b_coord, b_flux, b_var, b_prior = lax.optimization_barrier(
        (send, b_coord, b_flux, b_var, b_prior)
    )
    got = lax.all_to_all(
        send.reshape(devices, 16, TB), ("zone", "tile"), split_axis=0, concat_axis=0, tiled=True
    )
    own = jnp.concatenate(
        [b_coord, b_flux, b_var[None, :], b_prior[None, :], jnp.zeros_like(b_var)[None, :]], axis=0
    )
    inner = prepare_call(own)
    width = MB * TB
    ends = jnp.concatenate([own[:, -width:], own[:, :width]], axis=1)
    ends, *inner = lax.optimization_barrier((ends, *inner))
    up = [(i, i + 1) for i in range(zones - 1)]
    below = lax.ppermute(ends[:, :width], "zone", up)
    above = lax.ppermute(ends[:, width:], "zone", [(j, i) for i, j in up])
    edge = prepare_call(jnp.concatenate([below, above], axis=1))
    slots = devices * CAP
    result = match_call(got.reshape(devices * 16, TB), own, below, above, *inner, *edge)
    back = lax.all_to_all(result, ("zone", "tile"), split_axis=0, concat_axis=0, tiled=True)
    matched, prob = pl.pallas_call(
        unpack_kernel,
        out_shape=(
            jax.ShapeDtypeStruct((5, count * TB), F32),
            jax.ShapeDtypeStruct((count, TB), F32),
        ),
        in_specs=[SMEM, VMEM],
        out_specs=(VMEM, VMEM),
        compiler_params=params(16),
        name="unpack",
    )(place, back.reshape(slots * 6, TB))
    return matched, prob.reshape(count * TB)


def solution(mesh):
    both = ("zone", "tile")
    rows, columns, flat = P(both, None), P(None, both), P(both)
    return jax.shard_map(
        body,
        mesh=mesh,
        in_specs=(columns, flat, rows, rows, rows, columns, flat, flat, columns),
        out_specs=(columns, flat),
        check_vma=False,
    )
```

```python
import functools
import math

import jax
import jax.numpy as jnp
from jax import lax
from jax.experimental import pallas as pl
from jax.experimental.pallas import tpu as pltpu
from jax.sharding import PartitionSpec as P

TB = 128
K = 4
MB = 8
CAP = 4
UNROLL = 32
GROUP = 2
TERMS = 32
DEAD = 127
SHIFT = 17
SCALE = math.sqrt(0.5 / math.log(2.0))
F32 = jnp.float32
BF16 = jnp.bfloat16


def pack_kernel(dest, far_coord, far_var, labels, send, place, taken, a_coord, a_var, sems):
    devices = taken.shape[0]
    fetches = [
        pltpu.make_async_copy(far_coord, a_coord, sems.at[0]),
        pltpu.make_async_copy(far_var, a_var, sems.at[1]),
    ]
    for fetch in fetches:
        fetch.start()
    send[...] = jnp.zeros_like(send)

    def clear(i, c):
        taken[i] = 0
        return c

    lax.fori_loop(0, devices, clear, 0, unroll=8)
    for fetch in fetches:
        fetch.wait()

    def one(b, c):
        d = dest[b]
        r = taken[d]
        taken[d] = r + 1
        place[b] = d * (CAP * 6) + r * 6
        row = d * 16 + r * 4
        lanes = pl.ds(pl.multiple_of(b * TB, TB), TB)
        send[pl.ds(row, 1), :] = a_coord[0:1, lanes]
        send[pl.ds(row + 1, 1), :] = a_coord[1:2, lanes]
        send[pl.ds(row + 2, 1), :] = a_var[pl.ds(b, 1), :]
        send[pl.ds(row + 3, 1), :] = labels[pl.ds(b, 1), :]
        return c

    lax.fori_loop(0, dest.shape[0], one, 0, unroll=8)


def split(x):
    first = x.astype(BF16).astype(F32)
    second = (x - first).astype(BF16).astype(F32)
    return first, second, x - first - second


def left_terms(tile):
    u, v = tile[0:1] * SCALE, tile[1:2] * SCALE
    u, v, n = split(u), split(v), split(u * u + v * v)
    one = jnp.ones_like(u[0])
    zero = jnp.zeros_like(one)
    rows = [u[0], v[0], one, n[0], u[0], v[0], one, zero, u[0], v[0], one, zero]
    rows += [u[1], v[1], zero, n[1], u[1], v[1], zero, zero, u[2], v[2], zero, n[2]]
    return jnp.concatenate(rows + [jnp.zeros((TB - len(rows), TB), F32)], axis=0)


def right_terms(a_rows, right, m):
    row = lax.broadcasted_iota(jnp.int32, (8, TB), 0)
    upper, kind = row < 4, row & 3
    for half in range(CAP // 2):
        tile = a_rows[pl.ds(pl.multiple_of(m * 16 + 8 * half, 8), 8), :] * SCALE
        square = tile * tile
        square = pltpu.roll(square, 1, 0) + pltpu.roll(square, 2, 0)
        y = split(jnp.where(kind < 2, -2.0 * tile, jnp.where(kind == 2, square, 1.0)))
        z = [pltpu.roll(x, 4, 0) for x in y]
        for odd in range(2):
            y, z = (z, y) if odd else (y, z)
            parts = [jnp.where(upper, y[i], z[j]) for i, j in ((0, 1), (2, 0), (1, 0))]
            parts = jnp.concatenate(parts + [jnp.zeros((8, TB), F32)], axis=0)
            start = (m * CAP + 2 * half + odd) * TERMS
            right[pl.ds(pl.multiple_of(start, TERMS), TERMS), :] = parts.astype(BF16)


def sort_pairs(a_rows, order):
    messages = a_rows.shape[0] // 16
    line = lax.broadcasted_iota(jnp.int32, (TB, messages), 0).astype(F32)
    lane = lax.broadcasted_iota(jnp.int32, (1, messages), 1)
    keys = [None] * 16
    for r in range(CAP):
        turned = a_rows[pl.ds(4 * r + 3, messages, stride=16), :].T
        for k in range(K):
            keys[4 * k + r] = jnp.where(turned[K : K + 1] > k, turned[k : k + 1], float(DEAD))
    marks = [(line == key).astype(F32) for key in keys]
    here = functools.reduce(jnp.add, marks)
    before = lax.broadcasted_iota(jnp.int32, (TB, TB), 0) < lax.broadcasted_iota(jnp.int32, (TB, TB), 1)
    before = before.astype(F32)
    after = before.T.astype(BF16)
    both = jnp.concatenate([before, jnp.ones_like(before)], axis=1).astype(BF16)
    sums = jnp.dot(here.astype(BF16), both, preferred_element_type=F32)
    groups = jnp.floor((sums[:, TB:] + (GROUP - 1)) * (1.0 / GROUP))
    coarse = jnp.floor(groups * (1.0 / 16))
    first = 16.0 * jnp.dot(after, coarse.astype(BF16), preferred_element_type=F32)
    first = first + jnp.dot(after, (groups - 16.0 * coarse).astype(BF16), preferred_element_type=F32)
    place = sums[:, :TB] + GROUP * first
    for row in range(16):
        spot = jnp.sum(marks[row] * place, axis=0, keepdims=True)
        live = keys[row] < DEAD
        spot = jnp.where(live, spot, float(order_dump(messages))).astype(jnp.int32)
        code = (lane * CAP + row % 4) * TB + keys[row].astype(jnp.int32)
        order[row : row + 1, :] = spot * (1 << SHIFT) + code
        if row < 15:
            place = place + marks[row]
    order[16:17, :] = first[DEAD : DEAD + 1].astype(jnp.int32)


def order_dump(messages):
    return messages * CAP * K + 80 * (GROUP - 1) + GROUP * UNROLL


def list_size(messages):
    return order_dump(messages) + 1


def prepare_kernel(window, far_wide, far_left, wide, left, sems):
    runs = wide.shape[0] // 4

    def copies(run):
        part = pl.ds(run * 4, 4)
        return [
            pltpu.make_async_copy(near.at[part], there.at[part], sems.at[i, run])
            for i, (near, there) in enumerate(((wide, far_wide), (left, far_left)))
        ]

    def make(run, c):
        for k in range(4):
            w = run * 4 + k
            tile = window[:, pl.ds(pl.multiple_of(w * TB, TB), TB)]
            wide[w] = jnp.broadcast_to(-tile[5:6], (TB, TB)).T
            left[w] = left_terms(tile).T.astype(BF16)
        for copy in copies(run):
            copy.start()
        return c

    def end(run, c):
        for copy in copies(run):
            copy.wait()
        return c

    lax.fori_loop(0, runs, make, 0)
    lax.fori_loop(0, runs, end, 0)


def match_kernel(
    a_rows, own, below, above, wide_own, left_own, wide_edge, left_edge,
    out, window, wide, left, right, acc, order, blank, order_s, todo, sems,
):
    messages = a_rows.shape[0] // 16
    slots = messages * CAP
    blocks = own.shape[1] // TB
    row = lax.broadcasted_iota(jnp.int32, (8, TB), 0)
    fetches = []
    for edge, inner, there in ((wide_edge, wide_own, wide), (left_edge, left_own, left)):
        fetches.append((edge.at[0:MB], there.at[0:MB]))
        fetches.append((inner, there.at[MB : MB + blocks]))
        fetches.append((edge.at[MB : 2 * MB], there.at[MB + blocks : 2 * MB + blocks]))
    fetches.append((below, window.at[:, 0 : MB * TB]))
    fetches.append((own, window.at[:, MB * TB : (MB + blocks) * TB]))
    fetches.append((above, window.at[:, (MB + blocks) * TB : (2 * MB + blocks) * TB]))
    fetches = [pltpu.make_async_copy(a, b, sems.at[2 + i]) for i, (a, b) in enumerate(fetches)]
    for fetch in fetches:
        fetch.start()
    sort_pairs(a_rows, order)
    blank[...] = jnp.full(blank.shape, slots * TB, jnp.int32)
    copies = [
        pltpu.make_async_copy(order, order_s, sems.at[0]),
        pltpu.make_async_copy(blank, todo, sems.at[1]),
    ]
    for copy in copies:
        copy.start()
    acc[...] = jnp.zeros_like(acc)

    for copy in copies:
        copy.wait()

    def arrange(g, c):
        for m in range(messages):
            word = order_s[g, m]
            todo[lax.shift_right_logical(word, SHIFT)] = word
        for m in range(messages // 16):
            right_terms(a_rows, right, g * (messages // 16) + m)
        return c

    lax.fori_loop(0, 16, arrange, 0)
    for fetch in fetches:
        fetch.wait()
    groups = order_s[16, 0]

    def group(code):
        w = code[0] & (TB - 1)
        slot = [jnp.minimum(lax.shift_right_logical(c, 7), slots - 1) for c in code]
        tile = window[:, pl.ds(pl.multiple_of(w * TB, TB), TB)]

        terms = [right[pl.ds(pl.multiple_of(t * TERMS, TERMS), TERMS), :] for t in slot]
        terms = jnp.concatenate(terms, axis=1)
        apart = jnp.dot(left[w][:, :TERMS], terms, preferred_element_type=F32)
        spread = [jnp.broadcast_to(a_rows[pl.ds(4 * t + 2, 1), :], (8, TB)) for t in slot]
        high, low = [[] for _ in code], [[] for _ in code]
        for strip in range(0, TB, 16):
            s = [wide[w, strip + h : strip + h + 8, :] for h in (0, 8)]
            for e in range(GROUP):
                weight = []
                for h in range(2):
                    d2 = apart[strip + 8 * h : strip + 8 * h + 8, e * TB : (e + 1) * TB]
                    r = pltpu.reciprocal(s[h] - spread[e], approx=True)
                    weight.append(r * jnp.exp2(d2 * r))
                weight = jnp.concatenate(weight, axis=0)
                high[e].append(weight.astype(BF16))
                low[e].append((weight - high[e][-1].astype(F32)).astype(BF16))
        q = jnp.where(row == 5, -2.0, -2.0 * tile) * tile[6:7]
        q_high = q.astype(BF16).astype(F32)
        q = jnp.concatenate([q_high, q - q_high], axis=0).astype(BF16)
        q = jnp.concatenate([q, q], axis=1)
        total = []
        for e in range(GROUP):
            t = jnp.dot(q, jnp.concatenate(high[e] + low[e], axis=0), preferred_element_type=F32)
            total.append(t[0:8] + t[8:16])
        return total

    def chunk(c, carry):
        done = []
        for k in range(UNROLL):
            code = [todo[(c * UNROLL + k) * GROUP + e] & ((1 << SHIFT) - 1) for e in range(GROUP)]
            done.append((code, group(code)))
        for code, total in done:
            for e in range(GROUP):
                slot = lax.shift_right_logical(code[e], 7)
                acc[slot] = acc[slot] + total[e]
        return carry

    lax.fori_loop(0, (groups + UNROLL - 1) // UNROLL, chunk, 0)

    def finish(m, carry):
        parts = []
        for r in range(CAP):
            total = acc[m * CAP + r]
            parts.append((total / (1.0 + total[5:6]))[0:6])
        out[m] = jnp.concatenate(parts, axis=0)
        return carry

    lax.fori_loop(0, messages, finish, 0, unroll=2)


def unpack_kernel(place, back, matched, prob):
    def one(b, c):
        base = place[b]
        lanes = pl.ds(pl.multiple_of(b * TB, TB), TB)
        for q in range(5):
            matched[q : q + 1, lanes] = back[pl.ds(base + q, 1), :]
        prob[pl.ds(b, 1), :] = back[pl.ds(base + 5, 1), :]
        return c

    lax.fori_loop(0, place.shape[0], one, 0, unroll=8)


VMEM = pl.BlockSpec(memory_space=pltpu.VMEM)
FAR = pl.BlockSpec(memory_space=pltpu.HBM)
SMEM = pl.BlockSpec(memory_space=pltpu.SMEM)


def params(mib):
    return pltpu.CompilerParams(vmem_limit_bytes=mib * 2**20)


def far(*arrays):
    return [pltpu.with_memory_space_constraint(x, pltpu.HBM) for x in arrays]


def prepare_call(window):
    blocks = window.shape[1] // TB
    return pl.pallas_call(
        prepare_kernel,
        out_shape=(pltpu.HBM((blocks, TB, TB), F32), pltpu.HBM((blocks, TB, TB), BF16)),
        in_specs=[VMEM],
        out_specs=(FAR, FAR),
        scratch_shapes=[
            pltpu.VMEM((blocks, TB, TB), F32),
            pltpu.VMEM((blocks, TB, TB), BF16),
            pltpu.SemaphoreType.DMA((2, blocks // 4)),
        ],
        compiler_params=params(16),
        cost_estimate=pl.CostEstimate(flops=10**8, bytes_accessed=10**7, transcendentals=0),
        name="prepare",
    )(window)


def match_call(a_rows, own, below, above, *prepared):
    messages = a_rows.shape[0] // 16
    blocks = own.shape[1] // TB + 2 * MB
    size = -(-list_size(messages) // 1024) * 1024
    return pl.pallas_call(
        match_kernel,
        out_shape=jax.ShapeDtypeStruct((messages, CAP * 6, TB), F32),
        in_specs=[VMEM] + [FAR] * 7,
        out_specs=VMEM,
        scratch_shapes=[
            pltpu.VMEM((8, blocks * TB), F32),
            pltpu.VMEM((blocks, TB, TB), F32),
            pltpu.VMEM((blocks, TB, TB), BF16),
            pltpu.VMEM((messages * CAP * TERMS, TB), BF16),
            pltpu.VMEM((messages * CAP + 1, 8, TB), F32),
            pltpu.VMEM((24, messages), jnp.int32),
            pltpu.VMEM((size,), jnp.int32),
            pltpu.SMEM((24, messages), jnp.int32),
            pltpu.SMEM((size,), jnp.int32),
            pltpu.SemaphoreType.DMA((11,)),
        ],
        compiler_params=params(28),
        name="match",
    )(a_rows, *far(own, below, above, *prepared))


def body(a_coord, a_var, dest, cand, cand_count, b_coord, b_var, b_prior, b_flux):
    zones = lax.axis_size("zone")
    devices = zones * lax.axis_size("tile")
    count = dest.shape[0]
    labels = jnp.concatenate([cand, cand_count], axis=1).astype(F32)
    labels = jnp.pad(labels, ((0, 0), (0, TB - K - 1)))
    send, place = pl.pallas_call(
        pack_kernel,
        out_shape=(
            jax.ShapeDtypeStruct((devices * 16, TB), F32),
            jax.ShapeDtypeStruct((count,), jnp.int32),
        ),
        in_specs=[SMEM, FAR, FAR, VMEM],
        out_specs=(VMEM, SMEM),
        scratch_shapes=[
            pltpu.SMEM((devices,), jnp.int32),
            pltpu.VMEM(a_coord.shape, F32),
            pltpu.VMEM((count, TB), F32),
            pltpu.SemaphoreType.DMA((2,)),
        ],
        compiler_params=params(16),
        name="pack",
    )(dest.reshape(count), *far(a_coord, a_var.reshape(count, TB)), labels)
    send, b_coord, b_flux, b_var, b_prior = lax.optimization_barrier(
        (send, b_coord, b_flux, b_var, b_prior)
    )
    got = lax.all_to_all(
        send.reshape(devices, 16, TB), ("zone", "tile"), split_axis=0, concat_axis=0, tiled=True
    )
    own = jnp.concatenate(
        [b_coord, b_flux, b_var[None, :], b_prior[None, :], jnp.zeros_like(b_var)[None, :]], axis=0
    )
    inner = prepare_call(own)
    width = MB * TB
    ends = jnp.concatenate([own[:, -width:], own[:, :width]], axis=1)
    ends, *inner = lax.optimization_barrier((ends, *inner))
    up = [(i, i + 1) for i in range(zones - 1)]
    below = lax.ppermute(ends[:, :width], "zone", up)
    above = lax.ppermute(ends[:, width:], "zone", [(j, i) for i, j in up])
    edge = prepare_call(jnp.concatenate([below, above], axis=1))
    slots = devices * CAP
    result = match_call(got.reshape(devices * 16, TB), own, below, above, *inner, *edge)
    back = lax.all_to_all(result, ("zone", "tile"), split_axis=0, concat_axis=0, tiled=True)
    matched, prob = pl.pallas_call(
        unpack_kernel,
        out_shape=(
            jax.ShapeDtypeStruct((5, count * TB), F32),
            jax.ShapeDtypeStruct((count, TB), F32),
        ),
        in_specs=[SMEM, VMEM],
        out_specs=(VMEM, VMEM),
        compiler_params=params(16),
        name="unpack",
    )(place, back.reshape(slots * 6, TB))
    return matched, prob.reshape(count * TB)


def solution(mesh):
    both = ("zone", "tile")
    rows, columns, flat = P(both, None), P(None, both), P(both)
    return jax.shard_map(
        body,
        mesh=mesh,
        in_specs=(columns, flat, rows, rows, rows, columns, flat, flat, columns),
        out_specs=(columns, flat),
        check_vma=False,
    )
```

```python
import functools
import math

import jax
import jax.numpy as jnp
from jax import lax
from jax.experimental import pallas as pl
from jax.experimental.pallas import tpu as pltpu
from jax.sharding import PartitionSpec as P

TB = 128
K = 4
MB = 8
CAP = 4
UNROLL = 40
GROUP = 2
TERMS = 32
DEAD = 127
SHIFT = 17
SCALE = math.sqrt(0.5 / math.log(2.0))
F32 = jnp.float32
BF16 = jnp.bfloat16


def pack_kernel(dest, far_coord, far_var, labels, send, place, taken, a_coord, a_var, sems):
    devices = taken.shape[0]
    fetches = [
        pltpu.make_async_copy(far_coord, a_coord, sems.at[0]),
        pltpu.make_async_copy(far_var, a_var, sems.at[1]),
    ]
    for fetch in fetches:
        fetch.start()
    send[...] = jnp.zeros_like(send)

    def clear(i, c):
        taken[i] = 0
        return c

    lax.fori_loop(0, devices, clear, 0, unroll=8)
    for fetch in fetches:
        fetch.wait()

    def one(b, c):
        d = dest[b]
        r = taken[d]
        taken[d] = r + 1
        place[b] = d * (CAP * 6) + r * 6
        row = d * 16 + r * 4
        lanes = pl.ds(pl.multiple_of(b * TB, TB), TB)
        send[pl.ds(row, 1), :] = a_coord[0:1, lanes]
        send[pl.ds(row + 1, 1), :] = a_coord[1:2, lanes]
        send[pl.ds(row + 2, 1), :] = a_var[pl.ds(b, 1), :]
        send[pl.ds(row + 3, 1), :] = labels[pl.ds(b, 1), :]
        return c

    lax.fori_loop(0, dest.shape[0], one, 0, unroll=8)


def split(x):
    first = x.astype(BF16).astype(F32)
    second = (x - first).astype(BF16).astype(F32)
    return first, second, x - first - second


def left_terms(tile):
    u, v = tile[0:1] * SCALE, tile[1:2] * SCALE
    u, v, n = split(u), split(v), split(u * u + v * v)
    one = jnp.ones_like(u[0])
    zero = jnp.zeros_like(one)
    rows = [u[0], v[0], one, n[0], u[0], v[0], one, zero, u[0], v[0], one, zero]
    rows += [u[1], v[1], zero, n[1], u[1], v[1], zero, zero, u[2], v[2], zero, n[2]]
    return jnp.concatenate(rows + [jnp.zeros((TB - len(rows), TB), F32)], axis=0)


def right_terms(a_rows, right, m):
    row = lax.broadcasted_iota(jnp.int32, (8, TB), 0)
    upper, kind = row < 4, row & 3
    for half in range(CAP // 2):
        tile = a_rows[pl.ds(pl.multiple_of(m * 16 + 8 * half, 8), 8), :] * SCALE
        square = tile * tile
        square = pltpu.roll(square, 1, 0) + pltpu.roll(square, 2, 0)
        y = split(jnp.where(kind < 2, -2.0 * tile, jnp.where(kind == 2, square, 1.0)))
        z = [pltpu.roll(x, 4, 0) for x in y]
        for odd in range(2):
            y, z = (z, y) if odd else (y, z)
            parts = [jnp.where(upper, y[i], z[j]) for i, j in ((0, 1), (2, 0), (1, 0))]
            parts = jnp.concatenate(parts + [jnp.zeros((8, TB), F32)], axis=0)
            start = (m * CAP + 2 * half + odd) * TERMS
            right[pl.ds(pl.multiple_of(start, TERMS), TERMS), :] = parts.astype(BF16)


def sort_pairs(a_rows, order):
    messages = a_rows.shape[0] // 16
    line = lax.broadcasted_iota(jnp.int32, (TB, messages), 0).astype(F32)
    lane = lax.broadcasted_iota(jnp.int32, (1, messages), 1)
    keys = [None] * 16
    for r in range(CAP):
        turned = a_rows[pl.ds(4 * r + 3, messages, stride=16), :].T
        for k in range(K):
            keys[4 * k + r] = jnp.where(turned[K : K + 1] > k, turned[k : k + 1], float(DEAD))
    marks = [(line == key).astype(F32) for key in keys]
    here = functools.reduce(jnp.add, marks)
    before = lax.broadcasted_iota(jnp.int32, (TB, TB), 0) < lax.broadcasted_iota(jnp.int32, (TB, TB), 1)
    before = before.astype(F32)
    after = before.T.astype(BF16)
    both = jnp.concatenate([before, jnp.ones_like(before)], axis=1).astype(BF16)
    sums = jnp.dot(here.astype(BF16), both, preferred_element_type=F32)
    groups = jnp.floor((sums[:, TB:] + (GROUP - 1)) * (1.0 / GROUP))
    coarse = jnp.floor(groups * (1.0 / 16))
    first = 16.0 * jnp.dot(after, coarse.astype(BF16), preferred_element_type=F32)
    first = first + jnp.dot(after, (groups - 16.0 * coarse).astype(BF16), preferred_element_type=F32)
    place = sums[:, :TB] + GROUP * first
    for row in range(16):
        spot = jnp.sum(marks[row] * place, axis=0, keepdims=True)
        live = keys[row] < DEAD
        spot = jnp.where(live, spot, float(order_dump(messages))).astype(jnp.int32)
        code = (lane * CAP + row % 4) * TB + keys[row].astype(jnp.int32)
        order[row : row + 1, :] = spot * (1 << SHIFT) + code
        if row < 15:
            place = place + marks[row]
    order[16:17, :] = first[DEAD : DEAD + 1].astype(jnp.int32)


def order_dump(messages):
    return messages * CAP * K + 80 * (GROUP - 1) + GROUP * UNROLL


def list_size(messages):
    return order_dump(messages) + 1


def prepare_kernel(start, window, far_wide, far_left, wide, left, sems):
    runs = wide.shape[0] // 4

    def copies(run):
        part = pl.ds(run * 4, 4)
        return [
            pltpu.make_async_copy(near.at[part], there.at[part], sems.at[i, run])
            for i, (near, there) in enumerate(((wide, far_wide), (left, far_left)))
        ]

    def make(run, c):
        for k in range(4):
            w = run * 4 + k
            tile = window[:, pl.ds(pl.multiple_of((start + w) * TB, TB), TB)]
            wide[w] = jnp.broadcast_to(-tile[5:6], (TB, TB)).T
            left[w] = left_terms(tile).T.astype(BF16)
        for copy in copies(run):
            copy.start()
        return c

    def end(run, c):
        for copy in copies(run):
            copy.wait()
        return c

    lax.fori_loop(0, runs, make, 0)
    lax.fori_loop(0, runs, end, 0)


def match_kernel(
    a_rows, own, below, above, wide_first, left_first, wide_rest, left_rest, wide_edge, left_edge,
    out, window, wide, left, right, acc, order, blank, order_s, todo, sems,
):
    messages = a_rows.shape[0] // 16
    slots = messages * CAP
    blocks = own.shape[1] // TB
    row = lax.broadcasted_iota(jnp.int32, (8, TB), 0)
    fetches = []
    early = MB + left_first.shape[0]
    for edge, first, rest, there in (
        (wide_edge, wide_first, wide_rest, wide), (left_edge, left_first, left_rest, left)
    ):
        fetches.append((edge.at[0:MB], there.at[0:MB]))
        fetches.append((first, there.at[MB:early]))
        fetches.append((rest, there.at[early : MB + blocks]))
        fetches.append((edge.at[MB : 2 * MB], there.at[MB + blocks : 2 * MB + blocks]))
    fetches.append((below, window.at[:, 0 : MB * TB]))
    fetches.append((own, window.at[:, MB * TB : (MB + blocks) * TB]))
    fetches.append((above, window.at[:, (MB + blocks) * TB : (2 * MB + blocks) * TB]))
    fetches = [pltpu.make_async_copy(a, b, sems.at[2 + i]) for i, (a, b) in enumerate(fetches)]
    for fetch in fetches:
        fetch.start()
    sort_pairs(a_rows, order)
    blank[...] = jnp.full(blank.shape, slots * TB, jnp.int32)
    copies = [
        pltpu.make_async_copy(order, order_s, sems.at[0]),
        pltpu.make_async_copy(blank, todo, sems.at[1]),
    ]
    for copy in copies:
        copy.start()
    acc[...] = jnp.zeros_like(acc)

    for copy in copies:
        copy.wait()

    def arrange(g, c):
        for m in range(messages):
            word = order_s[g, m]
            todo[lax.shift_right_logical(word, SHIFT)] = word
        for m in range(messages // 16):
            right_terms(a_rows, right, g * (messages // 16) + m)
        return c

    lax.fori_loop(0, 16, arrange, 0)
    for fetch in fetches:
        fetch.wait()
    groups = order_s[16, 0]

    def group(code):
        w = code[0] & (TB - 1)
        slot = [jnp.minimum(lax.shift_right_logical(c, 7), slots - 1) for c in code]
        tile = window[:, pl.ds(pl.multiple_of(w * TB, TB), TB)]

        terms = [right[pl.ds(pl.multiple_of(t * TERMS, TERMS), TERMS), :] for t in slot]
        terms = jnp.concatenate(terms, axis=1)
        apart = jnp.dot(left[w][:, :TERMS], terms, preferred_element_type=F32)
        spread = [jnp.broadcast_to(a_rows[pl.ds(4 * t + 2, 1), :], (8, TB)) for t in slot]
        high, low = [[] for _ in code], [[] for _ in code]
        for strip in range(0, TB, 16):
            s = [wide[w, strip + h : strip + h + 8, :] for h in (0, 8)]
            for e in range(GROUP):
                weight = []
                for h in range(2):
                    d2 = apart[strip + 8 * h : strip + 8 * h + 8, e * TB : (e + 1) * TB]
                    r = pltpu.reciprocal(s[h] - spread[e], approx=True)
                    weight.append(r * jnp.exp2(d2 * r))
                weight = jnp.concatenate(weight, axis=0)
                high[e].append(weight.astype(BF16))
                low[e].append((weight - high[e][-1].astype(F32)).astype(BF16))
        q = jnp.where(row == 5, -2.0, -2.0 * tile) * tile[6:7]
        q_high = q.astype(BF16).astype(F32)
        q = jnp.concatenate([q_high, q - q_high], axis=0).astype(BF16)
        q = jnp.concatenate([q, q], axis=1)
        total = []
        for e in range(GROUP):
            t = jnp.dot(q, jnp.concatenate(high[e] + low[e], axis=0), preferred_element_type=F32)
            total.append(t[0:8] + t[8:16])
        return total

    def chunk(c, carry):
        done = []
        for k in range(UNROLL):
            code = [todo[(c * UNROLL + k) * GROUP + e] & ((1 << SHIFT) - 1) for e in range(GROUP)]
            done.append((code, group(code)))
        for code, total in done:
            for e in range(GROUP):
                slot = lax.shift_right_logical(code[e], 7)
                acc[slot] = acc[slot] + total[e]
        return carry

    lax.fori_loop(0, (groups + UNROLL - 1) // UNROLL, chunk, 0)

    def finish(m, carry):
        parts = []
        for r in range(CAP):
            total = acc[m * CAP + r]
            parts.append((total / (1.0 + total[5:6]))[0:6])
        out[m] = jnp.concatenate(parts, axis=0)
        return carry

    lax.fori_loop(0, messages, finish, 0, unroll=2)


def unpack_kernel(place, back, matched, prob):
    def one(b, c):
        base = place[b]
        lanes = pl.ds(pl.multiple_of(b * TB, TB), TB)
        for q in range(5):
            matched[q : q + 1, lanes] = back[pl.ds(base + q, 1), :]
        prob[pl.ds(b, 1), :] = back[pl.ds(base + 5, 1), :]
        return c

    lax.fori_loop(0, place.shape[0], one, 0, unroll=8)


VMEM = pl.BlockSpec(memory_space=pltpu.VMEM)
FAR = pl.BlockSpec(memory_space=pltpu.HBM)
SMEM = pl.BlockSpec(memory_space=pltpu.SMEM)


def params(mib):
    return pltpu.CompilerParams(vmem_limit_bytes=mib * 2**20)


def far(*arrays):
    return [pltpu.with_memory_space_constraint(x, pltpu.HBM) for x in arrays]


def prepare_call(window, start, blocks):
    return pl.pallas_call(
        functools.partial(prepare_kernel, start),
        out_shape=(pltpu.HBM((blocks, TB, TB), F32), pltpu.HBM((blocks, TB, TB), BF16)),
        in_specs=[VMEM],
        out_specs=(FAR, FAR),
        scratch_shapes=[
            pltpu.VMEM((blocks, TB, TB), F32),
            pltpu.VMEM((blocks, TB, TB), BF16),
            pltpu.SemaphoreType.DMA((2, blocks // 4)),
        ],
        compiler_params=params(16),
        cost_estimate=pl.CostEstimate(flops=10**8, bytes_accessed=10**7, transcendentals=0),
        name="prepare",
    )(window)


def match_call(a_rows, own, below, above, *prepared):
    messages = a_rows.shape[0] // 16
    blocks = own.shape[1] // TB + 2 * MB
    size = -(-list_size(messages) // 1024) * 1024
    return pl.pallas_call(
        match_kernel,
        out_shape=jax.ShapeDtypeStruct((messages, CAP * 6, TB), F32),
        in_specs=[VMEM] + [FAR] * 9,
        out_specs=VMEM,
        scratch_shapes=[
            pltpu.VMEM((8, blocks * TB), F32),
            pltpu.VMEM((blocks, TB, TB), F32),
            pltpu.VMEM((blocks, TB, TB), BF16),
            pltpu.VMEM((messages * CAP * TERMS, TB), BF16),
            pltpu.VMEM((messages * CAP + 1, 8, TB), F32),
            pltpu.VMEM((24, messages), jnp.int32),
            pltpu.VMEM((size,), jnp.int32),
            pltpu.SMEM((24, messages), jnp.int32),
            pltpu.SMEM((size,), jnp.int32),
            pltpu.SemaphoreType.DMA((13,)),
        ],
        compiler_params=params(28),
        name="match",
    )(a_rows, *far(own, below, above, *prepared))


def body(a_coord, a_var, dest, cand, cand_count, b_coord, b_var, b_prior, b_flux):
    zones = lax.axis_size("zone")
    devices = zones * lax.axis_size("tile")
    count = dest.shape[0]
    labels = jnp.concatenate([cand, cand_count], axis=1).astype(F32)
    labels = jnp.pad(labels, ((0, 0), (0, TB - K - 1)))
    send, place = pl.pallas_call(
        pack_kernel,
        out_shape=(
            jax.ShapeDtypeStruct((devices * 16, TB), F32),
            jax.ShapeDtypeStruct((count,), jnp.int32),
        ),
        in_specs=[SMEM, FAR, FAR, VMEM],
        out_specs=(VMEM, SMEM),
        scratch_shapes=[
            pltpu.SMEM((devices,), jnp.int32),
            pltpu.VMEM(a_coord.shape, F32),
            pltpu.VMEM((count, TB), F32),
            pltpu.SemaphoreType.DMA((2,)),
        ],
        compiler_params=params(16),
        name="pack",
    )(dest.reshape(count), *far(a_coord, a_var.reshape(count, TB)), labels)
    send, b_coord, b_flux, b_var, b_prior = lax.optimization_barrier(
        (send, b_coord, b_flux, b_var, b_prior)
    )
    got = lax.all_to_all(
        send.reshape(devices, 16, TB), ("zone", "tile"), split_axis=0, concat_axis=0, tiled=True
    )
    own = jnp.concatenate(
        [b_coord, b_flux, b_var[None, :], b_prior[None, :], jnp.zeros_like(b_var)[None, :]], axis=0
    )
    blocks, early = own.shape[1] // TB, 16
    first = prepare_call(own, 0, early)
    width = MB * TB
    ends = jnp.concatenate([own[:, -width:], own[:, :width]], axis=1)
    ends, *first = lax.optimization_barrier((ends, *first))
    up = [(i, i + 1) for i in range(zones - 1)]
    below = lax.ppermute(ends[:, :width], "zone", up)
    above = lax.ppermute(ends[:, width:], "zone", [(j, i) for i, j in up])
    rest = prepare_call(own, early, blocks - early)
    edge = prepare_call(jnp.concatenate([below, above], axis=1), 0, 2 * MB)
    slots = devices * CAP
    result = match_call(got.reshape(devices * 16, TB), own, below, above, *first, *rest, *edge)
    back = lax.all_to_all(result, ("zone", "tile"), split_axis=0, concat_axis=0, tiled=True)
    matched, prob = pl.pallas_call(
        unpack_kernel,
        out_shape=(
            jax.ShapeDtypeStruct((5, count * TB), F32),
            jax.ShapeDtypeStruct((count, TB), F32),
        ),
        in_specs=[SMEM, VMEM],
        out_specs=(VMEM, VMEM),
        compiler_params=params(16),
        name="unpack",
    )(place, back.reshape(slots * 6, TB))
    return matched, prob.reshape(count * TB)


def solution(mesh):
    both = ("zone", "tile")
    rows, columns, flat = P(both, None), P(None, both), P(both)
    return jax.shard_map(
        body,
        mesh=mesh,
        in_specs=(columns, flat, rows, rows, rows, columns, flat, flat, columns),
        out_specs=(columns, flat),
        check_vma=False,
    )
```

```python
import functools
import math

import jax
import jax.numpy as jnp
from jax import lax
from jax.experimental import pallas as pl
from jax.experimental.pallas import tpu as pltpu
from jax.sharding import PartitionSpec as P

TB = 128
K = 4
MB = 8
CAP = 4
UNROLL = 48
GROUP = 2
TERMS = 32
DEAD = 127
SHIFT = 17
SCALE = math.sqrt(0.5 / math.log(2.0))
F32 = jnp.float32
BF16 = jnp.bfloat16


def pack_kernel(dest, far_coord, far_var, labels, send, place, taken, a_coord, a_var, sems):
    devices = taken.shape[0]
    fetches = [
        pltpu.make_async_copy(far_coord, a_coord, sems.at[0]),
        pltpu.make_async_copy(far_var, a_var, sems.at[1]),
    ]
    for fetch in fetches:
        fetch.start()
    send[...] = jnp.zeros_like(send)

    def clear(i, c):
        taken[i] = 0
        return c

    lax.fori_loop(0, devices, clear, 0, unroll=8)
    for fetch in fetches:
        fetch.wait()

    def one(b, c):
        d = dest[b]
        r = taken[d]
        taken[d] = r + 1
        place[b] = d * (CAP * 6) + r * 6
        row = d * 16 + r * 4
        lanes = pl.ds(pl.multiple_of(b * TB, TB), TB)
        send[pl.ds(row, 1), :] = a_coord[0:1, lanes]
        send[pl.ds(row + 1, 1), :] = a_coord[1:2, lanes]
        send[pl.ds(row + 2, 1), :] = a_var[pl.ds(b, 1), :]
        send[pl.ds(row + 3, 1), :] = labels[pl.ds(b, 1), :]
        return c

    lax.fori_loop(0, dest.shape[0], one, 0, unroll=8)


def split(x):
    first = x.astype(BF16).astype(F32)
    second = (x - first).astype(BF16).astype(F32)
    return first, second, x - first - second


def left_terms(tile):
    u, v = tile[0:1] * SCALE, tile[1:2] * SCALE
    u, v, n = split(u), split(v), split(u * u + v * v)
    one = jnp.ones_like(u[0])
    zero = jnp.zeros_like(one)
    rows = [u[0], v[0], one, n[0], u[0], v[0], one, zero, u[0], v[0], one, zero]
    rows += [u[1], v[1], zero, n[1], u[1], v[1], zero, zero, u[2], v[2], zero, n[2]]
    return jnp.concatenate(rows + [jnp.zeros((TB - len(rows), TB), F32)], axis=0)


def right_terms(a_rows, right, m):
    row = lax.broadcasted_iota(jnp.int32, (8, TB), 0)
    upper, kind = row < 4, row & 3
    for half in range(CAP // 2):
        tile = a_rows[pl.ds(pl.multiple_of(m * 16 + 8 * half, 8), 8), :] * SCALE
        square = tile * tile
        square = pltpu.roll(square, 1, 0) + pltpu.roll(square, 2, 0)
        y = split(jnp.where(kind < 2, -2.0 * tile, jnp.where(kind == 2, square, 1.0)))
        z = [pltpu.roll(x, 4, 0) for x in y]
        for odd in range(2):
            y, z = (z, y) if odd else (y, z)
            parts = [jnp.where(upper, y[i], z[j]) for i, j in ((0, 1), (2, 0), (1, 0))]
            parts = jnp.concatenate(parts + [jnp.zeros((8, TB), F32)], axis=0)
            start = (m * CAP + 2 * half + odd) * TERMS
            right[pl.ds(pl.multiple_of(start, TERMS), TERMS), :] = parts.astype(BF16)


def sort_pairs(a_rows, order):
    messages = a_rows.shape[0] // 16
    line = lax.broadcasted_iota(jnp.int32, (TB, messages), 0).astype(F32)
    lane = lax.broadcasted_iota(jnp.int32, (1, messages), 1)
    keys = [None] * 16
    for r in range(CAP):
        turned = a_rows[pl.ds(4 * r + 3, messages, stride=16), :].T
        for k in range(K):
            keys[4 * k + r] = jnp.where(turned[K : K + 1] > k, turned[k : k + 1], float(DEAD))
    marks = [(line == key).astype(F32) for key in keys]
    here = functools.reduce(jnp.add, marks)
    before = lax.broadcasted_iota(jnp.int32, (TB, TB), 0) < lax.broadcasted_iota(jnp.int32, (TB, TB), 1)
    before = before.astype(F32)
    after = before.T.astype(BF16)
    both = jnp.concatenate([before, jnp.ones_like(before)], axis=1).astype(BF16)
    sums = jnp.dot(here.astype(BF16), both, preferred_element_type=F32)
    groups = jnp.floor((sums[:, TB:] + (GROUP - 1)) * (1.0 / GROUP))
    coarse = jnp.floor(groups * (1.0 / 16))
    first = 16.0 * jnp.dot(after, coarse.astype(BF16), preferred_element_type=F32)
    first = first + jnp.dot(after, (groups - 16.0 * coarse).astype(BF16), preferred_element_type=F32)
    place = sums[:, :TB] + GROUP * first
    for row in range(16):
        spot = jnp.sum(marks[row] * place, axis=0, keepdims=True)
        live = keys[row] < DEAD
        spot = jnp.where(live, spot, float(order_dump(messages))).astype(jnp.int32)
        code = (lane * CAP + row % 4) * TB + keys[row].astype(jnp.int32)
        order[row : row + 1, :] = spot * (1 << SHIFT) + code
        if row < 15:
            place = place + marks[row]
    order[16:17, :] = first[DEAD : DEAD + 1].astype(jnp.int32)


def order_dump(messages):
    return messages * CAP * K + 80 * (GROUP - 1) + GROUP * UNROLL


def list_size(messages):
    return order_dump(messages) + 1


def prepare_kernel(start, window, far_wide, far_left, wide, left, sems):
    runs = wide.shape[0] // 4

    def copies(run):
        part = pl.ds(run * 4, 4)
        return [
            pltpu.make_async_copy(near.at[part], there.at[part], sems.at[i, run])
            for i, (near, there) in enumerate(((wide, far_wide), (left, far_left)))
        ]

    def make(run, c):
        for k in range(4):
            w = run * 4 + k
            tile = window[:, pl.ds(pl.multiple_of((start + w) * TB, TB), TB)]
            wide[w] = jnp.broadcast_to(-tile[5:6], (TB, TB)).T
            left[w] = left_terms(tile).T.astype(BF16)
        for copy in copies(run):
            copy.start()
        return c

    def end(run, c):
        for copy in copies(run):
            copy.wait()
        return c

    lax.fori_loop(0, runs, make, 0)
    lax.fori_loop(0, runs, end, 0)


def match_kernel(
    a_rows, own, below, above, wide_first, left_first, wide_rest, left_rest, wide_edge, left_edge,
    out, window, wide, left, right, acc, order, blank, order_s, todo, sems,
):
    messages = a_rows.shape[0] // 16
    slots = messages * CAP
    blocks = own.shape[1] // TB
    row = lax.broadcasted_iota(jnp.int32, (8, TB), 0)
    fetches = []
    early = MB + left_first.shape[0]
    for edge, first, rest, there in (
        (wide_edge, wide_first, wide_rest, wide), (left_edge, left_first, left_rest, left)
    ):
        fetches.append((edge.at[0:MB], there.at[0:MB]))
        fetches.append((first, there.at[MB:early]))
        fetches.append((rest, there.at[early : MB + blocks]))
        fetches.append((edge.at[MB : 2 * MB], there.at[MB + blocks : 2 * MB + blocks]))
    fetches.append((below, window.at[:, 0 : MB * TB]))
    fetches.append((own, window.at[:, MB * TB : (MB + blocks) * TB]))
    fetches.append((above, window.at[:, (MB + blocks) * TB : (2 * MB + blocks) * TB]))
    fetches = [pltpu.make_async_copy(a, b, sems.at[2 + i]) for i, (a, b) in enumerate(fetches)]
    for fetch in fetches:
        fetch.start()
    sort_pairs(a_rows, order)
    blank[...] = jnp.full(blank.shape, slots * TB, jnp.int32)
    copies = [
        pltpu.make_async_copy(order, order_s, sems.at[0]),
        pltpu.make_async_copy(blank, todo, sems.at[1]),
    ]
    for copy in copies:
        copy.start()
    acc[...] = jnp.zeros_like(acc)

    for copy in copies:
        copy.wait()

    def arrange(g, c):
        for m in range(messages):
            word = order_s[g, m]
            todo[lax.shift_right_logical(word, SHIFT)] = word
        for m in range(messages // 16):
            right_terms(a_rows, right, g * (messages // 16) + m)
        return c

    lax.fori_loop(0, 16, arrange, 0)
    for fetch in fetches:
        fetch.wait()
    groups = order_s[16, 0]

    def group(code):
        w = code[0] & (TB - 1)
        slot = [jnp.minimum(lax.shift_right_logical(c, 7), slots - 1) for c in code]
        tile = window[:, pl.ds(pl.multiple_of(w * TB, TB), TB)]

        terms = [right[pl.ds(pl.multiple_of(t * TERMS, TERMS), TERMS), :] for t in slot]
        terms = jnp.concatenate(terms, axis=1)
        apart = jnp.dot(left[w][:, :TERMS], terms, preferred_element_type=F32)
        spread = [jnp.broadcast_to(a_rows[pl.ds(4 * t + 2, 1), :], (8, TB)) for t in slot]
        high, low = [[] for _ in code], [[] for _ in code]
        for strip in range(0, TB, 16):
            s = [wide[w, strip + h : strip + h + 8, :] for h in (0, 8)]
            for e in range(GROUP):
                weight = []
                for h in range(2):
                    d2 = apart[strip + 8 * h : strip + 8 * h + 8, e * TB : (e + 1) * TB]
                    r = pltpu.reciprocal(s[h] - spread[e], approx=True)
                    weight.append(r * jnp.exp2(d2 * r))
                weight = jnp.concatenate(weight, axis=0)
                high[e].append(weight.astype(BF16))
                low[e].append((weight - high[e][-1].astype(F32)).astype(BF16))
        q = jnp.where(row == 5, -2.0, -2.0 * tile) * tile[6:7]
        q_high = q.astype(BF16).astype(F32)
        q = jnp.concatenate([q_high, q - q_high], axis=0).astype(BF16)
        q = jnp.concatenate([q, q], axis=1)
        total = []
        for e in range(GROUP):
            t = jnp.dot(q, jnp.concatenate(high[e] + low[e], axis=0), preferred_element_type=F32)
            total.append(t[0:8] + t[8:16])
        return total

    def chunk(c, carry):
        done = []
        for k in range(UNROLL):
            code = [todo[(c * UNROLL + k) * GROUP + e] & ((1 << SHIFT) - 1) for e in range(GROUP)]
            done.append((code, group(code)))
        for code, total in done:
            for e in range(GROUP):
                slot = lax.shift_right_logical(code[e], 7)
                acc[slot] = acc[slot] + total[e]
        return carry

    lax.fori_loop(0, (groups + UNROLL - 1) // UNROLL, chunk, 0)

    def finish(m, carry):
        parts = []
        for r in range(CAP):
            total = acc[m * CAP + r]
            parts.append((total / (1.0 + total[5:6]))[0:6])
        out[m] = jnp.concatenate(parts, axis=0)
        return carry

    lax.fori_loop(0, messages, finish, 0, unroll=2)


def unpack_kernel(place, back, matched, prob):
    def one(b, c):
        base = place[b]
        lanes = pl.ds(pl.multiple_of(b * TB, TB), TB)
        for q in range(5):
            matched[q : q + 1, lanes] = back[pl.ds(base + q, 1), :]
        prob[pl.ds(b, 1), :] = back[pl.ds(base + 5, 1), :]
        return c

    lax.fori_loop(0, place.shape[0], one, 0, unroll=8)


VMEM = pl.BlockSpec(memory_space=pltpu.VMEM)
FAR = pl.BlockSpec(memory_space=pltpu.HBM)
SMEM = pl.BlockSpec(memory_space=pltpu.SMEM)


def params(mib):
    return pltpu.CompilerParams(vmem_limit_bytes=mib * 2**20)


def far(*arrays):
    return [pltpu.with_memory_space_constraint(x, pltpu.HBM) for x in arrays]


def prepare_call(window, start, blocks):
    return pl.pallas_call(
        functools.partial(prepare_kernel, start),
        out_shape=(pltpu.HBM((blocks, TB, TB), F32), pltpu.HBM((blocks, TB, TB), BF16)),
        in_specs=[VMEM],
        out_specs=(FAR, FAR),
        scratch_shapes=[
            pltpu.VMEM((blocks, TB, TB), F32),
            pltpu.VMEM((blocks, TB, TB), BF16),
            pltpu.SemaphoreType.DMA((2, blocks // 4)),
        ],
        compiler_params=params(16),
        cost_estimate=pl.CostEstimate(flops=10**8, bytes_accessed=10**7, transcendentals=0),
        name="prepare",
    )(window)


def match_call(a_rows, own, below, above, *prepared):
    messages = a_rows.shape[0] // 16
    blocks = own.shape[1] // TB + 2 * MB
    size = -(-list_size(messages) // 1024) * 1024
    return pl.pallas_call(
        match_kernel,
        out_shape=jax.ShapeDtypeStruct((messages, CAP * 6, TB), F32),
        in_specs=[VMEM] + [FAR] * 9,
        out_specs=VMEM,
        scratch_shapes=[
            pltpu.VMEM((8, blocks * TB), F32),
            pltpu.VMEM((blocks, TB, TB), F32),
            pltpu.VMEM((blocks, TB, TB), BF16),
            pltpu.VMEM((messages * CAP * TERMS, TB), BF16),
            pltpu.VMEM((messages * CAP + 1, 8, TB), F32),
            pltpu.VMEM((24, messages), jnp.int32),
            pltpu.VMEM((size,), jnp.int32),
            pltpu.SMEM((24, messages), jnp.int32),
            pltpu.SMEM((size,), jnp.int32),
            pltpu.SemaphoreType.DMA((13,)),
        ],
        compiler_params=params(28),
        name="match",
    )(a_rows, *far(own, below, above, *prepared))


def body(a_coord, a_var, dest, cand, cand_count, b_coord, b_var, b_prior, b_flux):
    zones = lax.axis_size("zone")
    devices = zones * lax.axis_size("tile")
    count = dest.shape[0]
    labels = jnp.concatenate([cand, cand_count], axis=1).astype(F32)
    labels = jnp.pad(labels, ((0, 0), (0, TB - K - 1)))
    send, place = pl.pallas_call(
        pack_kernel,
        out_shape=(
            jax.ShapeDtypeStruct((devices * 16, TB), F32),
            jax.ShapeDtypeStruct((count,), jnp.int32),
        ),
        in_specs=[SMEM, FAR, FAR, VMEM],
        out_specs=(VMEM, SMEM),
        scratch_shapes=[
            pltpu.SMEM((devices,), jnp.int32),
            pltpu.VMEM(a_coord.shape, F32),
            pltpu.VMEM((count, TB), F32),
            pltpu.SemaphoreType.DMA((2,)),
        ],
        compiler_params=params(16),
        name="pack",
    )(dest.reshape(count), *far(a_coord, a_var.reshape(count, TB)), labels)
    send, b_coord, b_flux, b_var, b_prior = lax.optimization_barrier(
        (send, b_coord, b_flux, b_var, b_prior)
    )
    got = lax.all_to_all(
        send.reshape(devices, 16, TB), ("zone", "tile"), split_axis=0, concat_axis=0, tiled=True
    )
    own = jnp.concatenate(
        [b_coord, b_flux, b_var[None, :], b_prior[None, :], jnp.zeros_like(b_var)[None, :]], axis=0
    )
    blocks, early = own.shape[1] // TB, 4
    first = prepare_call(own, 0, early)
    width = MB * TB
    ends = jnp.concatenate([own[:, -width:], own[:, :width]], axis=1)
    ends, *first = lax.optimization_barrier((ends, *first))
    up = [(i, i + 1) for i in range(zones - 1)]
    below = lax.ppermute(ends[:, :width], "zone", up)
    above = lax.ppermute(ends[:, width:], "zone", [(j, i) for i, j in up])
    rest = prepare_call(own, early, blocks - early)
    edge = prepare_call(jnp.concatenate([below, above], axis=1), 0, 2 * MB)
    slots = devices * CAP
    result = match_call(got.reshape(devices * 16, TB), own, below, above, *first, *rest, *edge)
    back = lax.all_to_all(result, ("zone", "tile"), split_axis=0, concat_axis=0, tiled=True)
    matched, prob = pl.pallas_call(
        unpack_kernel,
        out_shape=(
            jax.ShapeDtypeStruct((5, count * TB), F32),
            jax.ShapeDtypeStruct((count, TB), F32),
        ),
        in_specs=[SMEM, VMEM],
        out_specs=(VMEM, VMEM),
        compiler_params=params(16),
        name="unpack",
    )(place, back.reshape(slots * 6, TB))
    return matched, prob.reshape(count * TB)


def solution(mesh):
    both = ("zone", "tile")
    rows, columns, flat = P(both, None), P(None, both), P(both)
    return jax.shard_map(
        body,
        mesh=mesh,
        in_specs=(columns, flat, rows, rows, rows, columns, flat, flat, columns),
        out_specs=(columns, flat),
        check_vma=False,
    )
```

```python
import functools
import math

import jax
import jax.numpy as jnp
from jax import lax
from jax.experimental import pallas as pl
from jax.experimental.pallas import tpu as pltpu
from jax.sharding import PartitionSpec as P

TB = 128
K = 4
MB = 8
CAP = 4
UNROLL = 40
GROUP = 2
TERMS = 32
DEAD = 127
SHIFT = 17
SCALE = math.sqrt(0.5 / math.log(2.0))
F32 = jnp.float32
BF16 = jnp.bfloat16


def pack_kernel(dest, far_coord, far_var, labels, send, place, taken, a_coord, a_var, sems):
    devices = taken.shape[0]
    fetches = [
        pltpu.make_async_copy(far_coord, a_coord, sems.at[0]),
        pltpu.make_async_copy(far_var, a_var, sems.at[1]),
    ]
    for fetch in fetches:
        fetch.start()
    send[...] = jnp.zeros_like(send)

    def clear(i, c):
        taken[i] = 0
        return c

    lax.fori_loop(0, devices, clear, 0, unroll=8)
    for fetch in fetches:
        fetch.wait()

    def one(b, c):
        d = dest[b]
        r = taken[d]
        taken[d] = r + 1
        place[b] = d * (CAP * 6) + r * 6
        row = d * 16 + r * 4
        lanes = pl.ds(pl.multiple_of(b * TB, TB), TB)
        send[pl.ds(row, 1), :] = a_coord[0:1, lanes]
        send[pl.ds(row + 1, 1), :] = a_coord[1:2, lanes]
        send[pl.ds(row + 2, 1), :] = a_var[pl.ds(b, 1), :]
        send[pl.ds(row + 3, 1), :] = labels[pl.ds(b, 1), :]
        return c

    lax.fori_loop(0, dest.shape[0], one, 0, unroll=8)


def split(x):
    first = x.astype(BF16).astype(F32)
    second = (x - first).astype(BF16).astype(F32)
    return first, second, x - first - second


def left_terms(tile):
    u, v = tile[0:1] * SCALE, tile[1:2] * SCALE
    u, v, n = split(u), split(v), split(u * u + v * v)
    one = jnp.ones_like(u[0])
    zero = jnp.zeros_like(one)
    rows = [u[0], v[0], one, n[0], u[0], v[0], one, zero, u[0], v[0], one, zero]
    rows += [u[1], v[1], zero, n[1], u[1], v[1], zero, zero, u[2], v[2], zero, n[2]]
    return jnp.concatenate(rows + [jnp.zeros((TB - len(rows), TB), F32)], axis=0)


def right_terms(a_rows, right, m):
    row = lax.broadcasted_iota(jnp.int32, (8, TB), 0)
    upper, kind = row < 4, row & 3
    for half in range(CAP // 2):
        tile = a_rows[pl.ds(pl.multiple_of(m * 16 + 8 * half, 8), 8), :] * SCALE
        square = tile * tile
        square = pltpu.roll(square, 1, 0) + pltpu.roll(square, 2, 0)
        y = split(jnp.where(kind < 2, -2.0 * tile, jnp.where(kind == 2, square, 1.0)))
        z = [pltpu.roll(x, 4, 0) for x in y]
        for odd in range(2):
            y, z = (z, y) if odd else (y, z)
            parts = [jnp.where(upper, y[i], z[j]) for i, j in ((0, 1), (2, 0), (1, 0))]
            parts = jnp.concatenate(parts + [jnp.zeros((8, TB), F32)], axis=0)
            start = (m * CAP + 2 * half + odd) * TERMS
            right[pl.ds(pl.multiple_of(start, TERMS), TERMS), :] = parts.astype(BF16)


def sort_pairs(a_rows, order):
    messages = a_rows.shape[0] // 16
    line = lax.broadcasted_iota(jnp.int32, (TB, messages), 0).astype(F32)
    lane = lax.broadcasted_iota(jnp.int32, (1, messages), 1)
    keys = [None] * 16
    for r in range(CAP):
        turned = a_rows[pl.ds(4 * r + 3, messages, stride=16), :].T
        for k in range(K):
            keys[4 * k + r] = jnp.where(turned[K : K + 1] > k, turned[k : k + 1], float(DEAD))
    marks = [(line == key).astype(F32) for key in keys]
    here = functools.reduce(jnp.add, marks)
    before = lax.broadcasted_iota(jnp.int32, (TB, TB), 0) < lax.broadcasted_iota(jnp.int32, (TB, TB), 1)
    before = before.astype(F32)
    after = before.T.astype(BF16)
    both = jnp.concatenate([before, jnp.ones_like(before)], axis=1).astype(BF16)
    sums = jnp.dot(here.astype(BF16), both, preferred_element_type=F32)
    groups = jnp.floor((sums[:, TB:] + (GROUP - 1)) * (1.0 / GROUP))
    coarse = jnp.floor(groups * (1.0 / 16))
    first = 16.0 * jnp.dot(after, coarse.astype(BF16), preferred_element_type=F32)
    first = first + jnp.dot(after, (groups - 16.0 * coarse).astype(BF16), preferred_element_type=F32)
    place = sums[:, :TB] + GROUP * first
    for row in range(16):
        spot = jnp.sum(marks[row] * place, axis=0, keepdims=True)
        live = keys[row] < DEAD
        spot = jnp.where(live, spot, float(order_dump(messages))).astype(jnp.int32)
        code = (lane * CAP + row % 4) * TB + keys[row].astype(jnp.int32)
        order[row : row + 1, :] = spot * (1 << SHIFT) + code
        if row < 15:
            place = place + marks[row]
    order[16:17, :] = first[DEAD : DEAD + 1].astype(jnp.int32)


def order_dump(messages):
    return messages * CAP * K + 80 * (GROUP - 1) + GROUP * UNROLL


def list_size(messages):
    return order_dump(messages) + 1


def prepare_kernel(start, window, far_wide, far_left, wide, left, sems):
    runs = wide.shape[0] // 4

    def copies(run):
        part = pl.ds(run * 4, 4)
        return [
            pltpu.make_async_copy(near.at[part], there.at[part], sems.at[i, run])
            for i, (near, there) in enumerate(((wide, far_wide), (left, far_left)))
        ]

    def make(run, c):
        for k in range(4):
            w = run * 4 + k
            tile = window[:, pl.ds(pl.multiple_of((start + w) * TB, TB), TB)]
            wide[w] = jnp.broadcast_to(-tile[5:6], (TB, TB)).T
            left[w] = left_terms(tile).T.astype(BF16)
        for copy in copies(run):
            copy.start()
        return c

    def end(run, c):
        for copy in copies(run):
            copy.wait()
        return c

    lax.fori_loop(0, runs, make, 0)
    lax.fori_loop(0, runs, end, 0)


def match_kernel(
    a_rows, own, below, above, wide_first, left_first, wide_rest, left_rest, wide_edge, left_edge,
    out, window, wide, left, right, acc, order, blank, order_s, todo, sems,
):
    messages = a_rows.shape[0] // 16
    slots = messages * CAP
    blocks = own.shape[1] // TB
    row = lax.broadcasted_iota(jnp.int32, (8, TB), 0)
    fetches = []
    early = MB + left_first.shape[0]
    for edge, first, rest, there in (
        (wide_edge, wide_first, wide_rest, wide), (left_edge, left_first, left_rest, left)
    ):
        fetches.append((edge.at[0:MB], there.at[0:MB]))
        fetches.append((first, there.at[MB:early]))
        fetches.append((rest, there.at[early : MB + blocks]))
        fetches.append((edge.at[MB : 2 * MB], there.at[MB + blocks : 2 * MB + blocks]))
    fetches.append((below, window.at[:, 0 : MB * TB]))
    fetches.append((own, window.at[:, MB * TB : (MB + blocks) * TB]))
    fetches.append((above, window.at[:, (MB + blocks) * TB : (2 * MB + blocks) * TB]))
    fetches = [pltpu.make_async_copy(a, b, sems.at[2 + i]) for i, (a, b) in enumerate(fetches)]
    for fetch in fetches:
        fetch.start()
    sort_pairs(a_rows, order)
    blank[...] = jnp.full(blank.shape, slots * TB, jnp.int32)
    copies = [
        pltpu.make_async_copy(order, order_s, sems.at[0]),
        pltpu.make_async_copy(blank, todo, sems.at[1]),
    ]
    for copy in copies:
        copy.start()
    acc[...] = jnp.zeros_like(acc)

    for copy in copies:
        copy.wait()

    def arrange(g, c):
        for m in range(messages):
            word = order_s[g, m]
            todo[lax.shift_right_logical(word, SHIFT)] = word
        for m in range(messages // 16):
            right_terms(a_rows, right, g * (messages // 16) + m)
        return c

    lax.fori_loop(0, 16, arrange, 0)
    for fetch in fetches:
        fetch.wait()
    groups = order_s[16, 0]

    def group(code):
        w = code[0] & (TB - 1)
        slot = [jnp.minimum(lax.shift_right_logical(c, 7), slots - 1) for c in code]
        tile = window[:, pl.ds(pl.multiple_of(w * TB, TB), TB)]

        terms = [right[pl.ds(pl.multiple_of(t * TERMS, TERMS), TERMS), :] for t in slot]
        terms = jnp.concatenate(terms, axis=1)
        apart = jnp.dot(left[w][:, :TERMS], terms, preferred_element_type=F32)
        spread = [jnp.broadcast_to(a_rows[pl.ds(4 * t + 2, 1), :], (8, TB)) for t in slot]
        high, low = [[] for _ in code], [[] for _ in code]
        for strip in range(0, TB, 16):
            s = [wide[w, strip + h : strip + h + 8, :] for h in (0, 8)]
            for e in range(GROUP):
                weight = []
                for h in range(2):
                    d2 = apart[strip + 8 * h : strip + 8 * h + 8, e * TB : (e + 1) * TB]
                    r = pltpu.reciprocal(s[h] - spread[e], approx=True)
                    weight.append(r * jnp.exp2(d2 * r))
                weight = jnp.concatenate(weight, axis=0)
                high[e].append(weight.astype(BF16))
                low[e].append((weight - high[e][-1].astype(F32)).astype(BF16))
        q = jnp.where(row == 5, -2.0, -2.0 * tile) * tile[6:7]
        q_high = q.astype(BF16).astype(F32)
        q = jnp.concatenate([q_high, q - q_high], axis=0).astype(BF16)
        q = jnp.concatenate([q, q], axis=1)
        total = []
        for e in range(GROUP):
            t = jnp.dot(q, jnp.concatenate(high[e] + low[e], axis=0), preferred_element_type=F32)
            total.append(t[0:8] + t[8:16])
        return total

    def chunk(c, carry):
        done = []
        for k in range(UNROLL):
            code = [todo[(c * UNROLL + k) * GROUP + e] & ((1 << SHIFT) - 1) for e in range(GROUP)]
            done.append((code, group(code)))
        for code, total in done:
            for e in range(GROUP):
                slot = lax.shift_right_logical(code[e], 7)
                acc[slot] = acc[slot] + total[e]
        return carry

    lax.fori_loop(0, (groups + UNROLL - 1) // UNROLL, chunk, 0)

    def finish(m, carry):
        parts = []
        for r in range(CAP):
            total = acc[m * CAP + r]
            parts.append((total / (1.0 + total[5:6]))[0:6])
        out[m] = jnp.concatenate(parts, axis=0)
        return carry

    lax.fori_loop(0, messages, finish, 0, unroll=8)


def unpack_kernel(place, back, matched, prob):
    def one(b, c):
        base = place[b]
        lanes = pl.ds(pl.multiple_of(b * TB, TB), TB)
        for q in range(5):
            matched[q : q + 1, lanes] = back[pl.ds(base + q, 1), :]
        prob[pl.ds(b, 1), :] = back[pl.ds(base + 5, 1), :]
        return c

    lax.fori_loop(0, place.shape[0], one, 0, unroll=16)


VMEM = pl.BlockSpec(memory_space=pltpu.VMEM)
FAR = pl.BlockSpec(memory_space=pltpu.HBM)
SMEM = pl.BlockSpec(memory_space=pltpu.SMEM)


def params(mib):
    return pltpu.CompilerParams(vmem_limit_bytes=mib * 2**20)


def far(*arrays):
    return [pltpu.with_memory_space_constraint(x, pltpu.HBM) for x in arrays]


def prepare_call(window, start, blocks):
    return pl.pallas_call(
        functools.partial(prepare_kernel, start),
        out_shape=(pltpu.HBM((blocks, TB, TB), F32), pltpu.HBM((blocks, TB, TB), BF16)),
        in_specs=[VMEM],
        out_specs=(FAR, FAR),
        scratch_shapes=[
            pltpu.VMEM((blocks, TB, TB), F32),
            pltpu.VMEM((blocks, TB, TB), BF16),
            pltpu.SemaphoreType.DMA((2, blocks // 4)),
        ],
        compiler_params=params(16),
        cost_estimate=pl.CostEstimate(flops=10**8, bytes_accessed=10**7, transcendentals=0),
        name="prepare",
    )(window)


def match_call(a_rows, own, below, above, *prepared):
    messages = a_rows.shape[0] // 16
    blocks = own.shape[1] // TB + 2 * MB
    size = -(-list_size(messages) // 1024) * 1024
    return pl.pallas_call(
        match_kernel,
        out_shape=jax.ShapeDtypeStruct((messages, CAP * 6, TB), F32),
        in_specs=[VMEM] + [FAR] * 9,
        out_specs=VMEM,
        scratch_shapes=[
            pltpu.VMEM((8, blocks * TB), F32),
            pltpu.VMEM((blocks, TB, TB), F32),
            pltpu.VMEM((blocks, TB, TB), BF16),
            pltpu.VMEM((messages * CAP * TERMS, TB), BF16),
            pltpu.VMEM((messages * CAP + 1, 8, TB), F32),
            pltpu.VMEM((24, messages), jnp.int32),
            pltpu.VMEM((size,), jnp.int32),
            pltpu.SMEM((24, messages), jnp.int32),
            pltpu.SMEM((size,), jnp.int32),
            pltpu.SemaphoreType.DMA((13,)),
        ],
        compiler_params=params(28),
        name="match",
    )(a_rows, *far(own, below, above, *prepared))


def body(a_coord, a_var, dest, cand, cand_count, b_coord, b_var, b_prior, b_flux):
    zones = lax.axis_size("zone")
    devices = zones * lax.axis_size("tile")
    count = dest.shape[0]
    labels = jnp.concatenate([cand, cand_count], axis=1).astype(F32)
    labels = jnp.pad(labels, ((0, 0), (0, TB - K - 1)))
    send, place = pl.pallas_call(
        pack_kernel,
        out_shape=(
            jax.ShapeDtypeStruct((devices * 16, TB), F32),
            jax.ShapeDtypeStruct((count,), jnp.int32),
        ),
        in_specs=[SMEM, FAR, FAR, VMEM],
        out_specs=(VMEM, SMEM),
        scratch_shapes=[
            pltpu.SMEM((devices,), jnp.int32),
            pltpu.VMEM(a_coord.shape, F32),
            pltpu.VMEM((count, TB), F32),
            pltpu.SemaphoreType.DMA((2,)),
        ],
        compiler_params=params(16),
        name="pack",
    )(dest.reshape(count), *far(a_coord, a_var.reshape(count, TB)), labels)
    send, b_coord, b_flux, b_var, b_prior = lax.optimization_barrier(
        (send, b_coord, b_flux, b_var, b_prior)
    )
    got = lax.all_to_all(
        send.reshape(devices, 16, TB), ("zone", "tile"), split_axis=0, concat_axis=0, tiled=True
    )
    own = jnp.concatenate(
        [b_coord, b_flux, b_var[None, :], b_prior[None, :], jnp.zeros_like(b_var)[None, :]], axis=0
    )
    blocks, early = own.shape[1] // TB, 16
    first = prepare_call(own, 0, early)
    width = MB * TB
    ends = jnp.concatenate([own[:, -width:], own[:, :width]], axis=1)
    ends, *first = lax.optimization_barrier((ends, *first))
    up = [(i, i + 1) for i in range(zones - 1)]
    below = lax.ppermute(ends[:, :width], "zone", up)
    above = lax.ppermute(ends[:, width:], "zone", [(j, i) for i, j in up])
    rest = prepare_call(own, early, blocks - early)
    edge = prepare_call(jnp.concatenate([below, above], axis=1), 0, 2 * MB)
    slots = devices * CAP
    result = match_call(got.reshape(devices * 16, TB), own, below, above, *first, *rest, *edge)
    back = lax.all_to_all(result, ("zone", "tile"), split_axis=0, concat_axis=0, tiled=True)
    matched, prob = pl.pallas_call(
        unpack_kernel,
        out_shape=(
            jax.ShapeDtypeStruct((5, count * TB), F32),
            jax.ShapeDtypeStruct((count, TB), F32),
        ),
        in_specs=[SMEM, VMEM],
        out_specs=(VMEM, VMEM),
        compiler_params=params(16),
        name="unpack",
    )(place, back.reshape(slots * 6, TB))
    return matched, prob.reshape(count * TB)


def solution(mesh):
    both = ("zone", "tile")
    rows, columns, flat = P(both, None), P(None, both), P(both)
    return jax.shard_map(
        body,
        mesh=mesh,
        in_specs=(columns, flat, rows, rows, rows, columns, flat, flat, columns),
        out_specs=(columns, flat),
        check_vma=False,
    )
```
